512 devices in a mesh: leaf: 32 (over z, x_lo, core), panel: 16 (over y, x_hi).
Axes of the slice: x: 4 (x_hi: 2, x_lo: 2; x = x_hi * 2 + x_lo), y: 8, z: 8, core: 2. Of those that a mesh axis runs over, the one named last changes fastest.
Arguments:
- child_update: float32 [32, 12, 128, 1536], P('leaf', None, 'panel'), may hold values from -1 to 5, as said below
- separator_columns: float32 [2, 32, 16, 128, 512], P(None, 'leaf', None, 'panel'), may hold values from -1 to 5, as said below
- placement: int32 [2, 32, 12], replicated, may hold values from 0 to 15, as said below
Outputs:
- factors: float32 [2, 32, 16, 128, 512], P(None, 'leaf', None, 'panel')
- top_update: float32 [32, 12, 128, 1536], P('leaf', None, 'panel')
The draws below stay inside these ranges and needn't reach their ends.
Inputs may be any that keep to these rules, and one draw needn't show every extreme that they name: For each level k and leaf index l, placement[k, l] holds 12 distinct block numbers; where l // 2**k is odd they are the numbers 4 to 15 in some order. `child_update`: each leaf index's matrix is symmetric positive definite. `separator_columns`: for each level and leaf index, the first 512 rows form a symmetric positive definite matrix, and every front assembled by the steps has a positive definite separator block.
All inputs are finite; a program needn't handle non-finite values.
Results may differ from the reference program's by a relative error of at most 0.0001.
Values sent between devices are 32-bit elements; how exact they have to be, the bound alone decides.
No kernel may reach another device: no remote copies, remote signals or barrier semaphores. Data moves between devices by JAX's collectives and lax.ppermute only.
A program may use at most 64 MiB of HBM per device.

```python
import math
import jax
import jax.numpy as jnp
from jax import lax

F = 2048
S = 512
LEVELS = 2
U = 1536
FB = 16
SB = 4
UB = 12
N_LEAF = 32


def draw_child_update(key, part):
    subkeys = jax.random.split(key, 2)
    entries = jax.random.uniform(subkeys[0], (N_LEAF, U, U), jnp.float32, -1.0, 1.0) * (0.75 / math.sqrt(U))
    diagonal_vals = jnp.exp(jax.random.uniform(subkeys[1], (N_LEAF, U), jnp.float32, math.log(3.0), math.log(5.0)))
    symmetric = (entries + jnp.swapaxes(entries, 1, 2)) * 0.7071
    identity = jnp.eye(U, dtype=jnp.float32)
    matrix = symmetric * (1.0 - identity) + identity * diagonal_vals[:, None, :]
    return matrix.reshape(N_LEAF, UB, 128, U).astype(jnp.float32)


def draw_separator_columns(key, part):
    subkeys = jax.random.split(key, 6)
    noise_scale = 0.25 / (math.sqrt(U) + math.sqrt(S))
    shared_scale = math.sqrt(0.3) / (math.sqrt(U // 2) + math.sqrt(S))
    perm_keys = jax.random.split(subkeys[4], LEVELS * N_LEAF)
    shuffled = jax.vmap(lambda subkey: jax.random.permutation(subkey, jnp.arange(U, dtype=jnp.int32)))(perm_keys)
    partner_group = shuffled // 2
    offsets = jnp.arange(LEVELS * N_LEAF, dtype=jnp.int32)[:, None] * (U // 2)
    flat_index = (partner_group + offsets).reshape(-1)
    row_signs = (2 * jax.random.randint(subkeys[5], (LEVELS, N_LEAF, U), 0, 2) - 1).astype(jnp.float32)
    square = jax.random.uniform(subkeys[0], (LEVELS, N_LEAF, S, S), jnp.float32, -1.0, 1.0) * (0.75 / math.sqrt(S))
    noise_part = jax.random.uniform(subkeys[1], (LEVELS, N_LEAF, U, S), jnp.float32, -1.0, 1.0) * (noise_scale * math.sqrt(3.0))
    shared = jax.random.uniform(subkeys[2], (LEVELS, N_LEAF, U // 2, S), jnp.float32, -1.0, 1.0) * (shared_scale * math.sqrt(3.0))
    pivots = jnp.exp(jax.random.uniform(subkeys[3], (LEVELS, N_LEAF, S), jnp.float32, math.log(2.5), math.log(5.0)))
    picked = shared.reshape(LEVELS * N_LEAF * (U // 2), S)[flat_index].reshape(LEVELS, N_LEAF, U, S)
    lower_part = noise_part + row_signs[:, :, :, None] * picked
    symmetric = (square + jnp.swapaxes(square, 2, 3)) * 0.7071
    identity = jnp.eye(S, dtype=jnp.float32)
    top_block = symmetric * (1.0 - identity) + identity * pivots[:, :, None, :]
    matrix = jnp.concatenate([top_block, lower_part], axis=2)
    return matrix.reshape(LEVELS, N_LEAF, FB, 128, S).astype(jnp.float32)


def draw_placement(key, part):
    left_keys = jax.random.split(jax.random.fold_in(key, 11), LEVELS * N_LEAF)
    right_keys = jax.random.split(jax.random.fold_in(key, 23), LEVELS * N_LEAF)
    left_lists = jax.vmap(lambda subkey: jax.random.permutation(subkey, jnp.arange(FB, dtype=jnp.int32))[:UB])(left_keys)
    right_lists = jax.vmap(lambda subkey: SB + jax.random.permutation(subkey, jnp.arange(UB, dtype=jnp.int32)))(right_keys)
    left_lists = left_lists.reshape(LEVELS, N_LEAF, UB)
    right_lists = right_lists.reshape(LEVELS, N_LEAF, UB)
    levels_idx = jnp.arange(LEVELS, dtype=jnp.int32)[:, None]
    leaves_idx = jnp.arange(N_LEAF, dtype=jnp.int32)[None, :]
    is_right = leaves_idx // 2 ** levels_idx % 2 == 1
    return jnp.where(is_right[:, :, None], right_lists, left_lists).astype(jnp.int32)


def setup_inputs(seed: int = 0) -> dict:
    keys = jax.random.split(jax.random.key(seed), 4)
    child_update = draw_child_update(jax.random.fold_in(keys[3], 71), 0)
    separator_columns = draw_separator_columns(jax.random.fold_in(keys[3], 71), 0)
    placement = draw_placement(jax.random.fold_in(keys[3], 71), 0)
    return dict(child_update=child_update, separator_columns=separator_columns, placement=placement)


def extend(own_update, block_place):
    onehot = (block_place[:, None] == jnp.arange(FB, dtype=jnp.int32)[None, :]).astype(jnp.float32)
    blocked = own_update.reshape(UB, 128, UB, 128)
    moved_cols = jnp.einsum('aibc,bk->aikc', blocked, onehot, precision=lax.Precision.HIGHEST)
    placed = jnp.einsum('aikc,aj->jikc', moved_cols, onehot, precision=lax.Precision.HIGHEST)
    return placed.reshape(F, F)

def reference(child_update, separator_columns, placement):
    updates = [child_update[idx].reshape(U, U) for idx in range(N_LEAF)]
    factor_levels = []
    for merge_level in range(LEVELS):
        spacing = 2 ** merge_level
        level_rows = []
        new_updates = list(updates)
        for head_leaf in range(N_LEAF):
            if head_leaf % (2 * spacing) == 0:
                front_rows = extend(updates[head_leaf], placement[merge_level, head_leaf])
                front_rows = front_rows + extend(updates[head_leaf + spacing], placement[merge_level, head_leaf + spacing])
                front_rows = front_rows.at[:, :S].add(separator_columns[merge_level, head_leaf].reshape(F, S))
                pivot_factor = jnp.linalg.cholesky(front_rows[:S, :S])
                factor_below = jax.scipy.linalg.solve_triangular(pivot_factor, front_rows[S:, :S].T, lower=True).T
                factor_rows = jnp.concatenate([pivot_factor, factor_below], axis=0)
                level_rows.append(factor_rows.reshape(FB, 128, S))
                new_updates[head_leaf] = front_rows[S:, S:] - jnp.dot(factor_below, factor_below.T, precision=lax.Precision.HIGHEST)
            else:
                level_rows.append(jnp.zeros((FB, 128, S), jnp.float32))
        updates = new_updates
        factor_levels.append(jnp.stack(level_rows))
    factors = jnp.stack(factor_levels)
    top_rows = []
    for head_leaf in range(N_LEAF):
        if head_leaf % 2 ** LEVELS == 0:
            top_rows.append(updates[head_leaf].reshape(UB, 128, U))
        else:
            top_rows.append(jnp.zeros((UB, 128, U), jnp.float32))
    return (factors, jnp.stack(top_rows))
```

```python
import jax
import jax.numpy as jnp
from jax import lax
from jax.experimental import pallas as pl
from jax.experimental.pallas import tpu as pltpu
from jax.sharding import Mesh
from jax.sharding import PartitionSpec as P

F = 2048
S = 512
U = 1536
FB = 16
SB = 4
UB = 12
ROWS = 8
BLOCK = 32
HALF = 16
HI = lax.Precision.HIGHEST
AXES = ("z", "xlo", "core", "y", "xhi")
LEAF = ("z", "xlo", "core")
PANEL = ("y", "xhi")
UPPER = [(a, b) for a in range(SB) for b in range(a, SB)]
VMEM_LIMIT = 48 << 20


def nt(a, b):
    return lax.dot_general(
        a, b, (((1,), (1,)), ((), ())), precision=HI, preferred_element_type=jnp.float32
    )


def nn(a, b):
    return jnp.dot(a, b, precision=HI, preferred_element_type=jnp.float32)


def spread_row(tile, row):
    return jnp.broadcast_to(tile[row : row + 1, :], tile.shape)


def split3(x):
    high = x.astype(jnp.bfloat16)
    rest = x - high.astype(jnp.float32)
    mid = rest.astype(jnp.bfloat16)
    low = (rest - mid.astype(jnp.float32)).astype(jnp.bfloat16)
    return high, mid, low


def factor_block(m_ref, start):
    tile, lo = start // 128, start % 128
    groups, cols = BLOCK // 8, S // 128
    lane = lax.broadcasted_iota(jnp.int32, (8, 128), 1)
    sub = lax.broadcasted_iota(jnp.int32, (8, 128), 0)
    rows = [
        [m_ref[start + 8 * g : start + 8 * g + 8, 128 * c : 128 * c + 128] for c in range(cols)]
        for g in range(groups)
    ]
    diag = [rows[g][tile] for g in range(groups)]
    inside = (lane >= lo) & (lane < lo + BLOCK)
    for g in range(groups):
        unit = jnp.where(lane == sub + (lo + 8 * g), 1.0, 0.0)
        rows[g][tile] = jnp.where(inside, unit, diag[g])
    factor = [jnp.zeros((8, 128), jnp.float32) for _ in range(groups)]
    for first in range(0, BLOCK, HALF):
        spread = {
            k: {
                g: jnp.broadcast_to(diag[g][:, lo + k : lo + k + 1], (8, 128))
                for g in range(k // 8, groups)
            }
            for k in range(first, first + HALF)
        }
        last = first + HALF == BLOCK
        for j in range(first, first + HALF):
            gj, s = j // 8, j % 8
            inv = lax.rsqrt(spread_row(spread[j][gj], s))
            col = {g: spread[j][g] * inv for g in range(gj, groups)}
            for k in range(j + 1, first + HALF):
                w = spread_row(col[k // 8], k % 8)
                for g in range(k // 8, groups):
                    spread[k][g] = spread[k][g] - col[g] * w
            below = jnp.where(sub > s, col[gj], 0.0)
            factor[gj] = jnp.where((lane == lo + j) & (sub >= s), col[gj], factor[gj])
            for g in range(gj + 1, groups):
                factor[g] = jnp.where(lane == lo + j, col[g], factor[g])
            for c in range(cols):
                u = spread_row(rows[gj][c], s) * inv
                rows[gj][c] = jnp.where(sub == s, u, rows[gj][c] - below * u)
                for g in range(gj + 1, groups):
                    rows[g][c] = rows[g][c] - col[g] * u
            if not last:
                u = spread_row(diag[gj], s) * inv
                diag[gj] = jnp.where(sub == s, u, diag[gj] - below * u)
                for g in range(gj + 1, groups):
                    diag[g] = diag[g] - col[g] * u
    joined = [jnp.concatenate([rows[g][c] for g in range(groups)], 0) for c in range(cols)]
    return joined, jnp.concatenate(factor, 0)


def factorize(m_ref, l_ref, inv_ref, u_ref):
    cols = S // 128
    lane = lax.broadcasted_iota(jnp.int32, (BLOCK, 128), 1)
    for start in range(0, S, BLOCK):
        end, tile, lo = start + BLOCK, start // 128, start % 128
        rows, diag = factor_block(m_ref, start)
        for c in range(cols):
            if c < tile:
                value = rows[c]
            elif c == tile:
                value = jnp.where(lane < lo + BLOCK, rows[c], 0.0)
            else:
                value = jnp.zeros_like(rows[c])
            inv_ref[start:end, 128 * c : 128 * c + 128] = value
        upper = [jnp.where(lane >= lo + BLOCK, rows[tile], 0.0)] + rows[tile + 1 :]
        for i, value in enumerate(upper):
            c = tile + i
            u_ref[lo : lo + BLOCK, 128 * c : 128 * c + 128] = value
        l_ref[start:end, 128 * tile : 128 * tile + 128] = diag
        if end < S:
            skip = end // 128 - tile
            left = split3(jnp.concatenate(upper[skip:], 1))
            right = split3(jnp.concatenate(rows, 1))
            pairs = ((0, 0), (0, 1), (1, 0), (1, 1), (0, 2), (2, 0))
            update = lax.dot_general(
                jnp.concatenate([left[a] for a, _ in pairs], 0),
                jnp.concatenate([right[b] for _, b in pairs], 0),
                (((0,), (0,)), ((), ())),
                preferred_element_type=jnp.float32,
            )
            offset = end % 128 if skip == 0 else 0
            for c in range(cols):
                value = m_ref[end:S, 128 * c : 128 * c + 128]
                if c == tile:
                    at = lax.broadcasted_iota(jnp.int32, value.shape, 1)
                    value = jnp.where((at >= lo) & (at < lo + BLOCK), 0.0, value)
                m_ref[end:S, 128 * c : 128 * c + 128] = (
                    value - update[offset:, 128 * c : 128 * c + 128]
                )
        if end % 128 == 0:
            at = slice(128 * tile, 128 * tile + 128)
            for c in range(cols):
                if c < tile:
                    l_ref[128 * c : 128 * c + 128, at] = jnp.zeros((128, 128), jnp.float32)
                else:
                    turned = u_ref[:, 128 * c : 128 * c + 128].T
                    if c == tile:
                        turned = turned + l_ref[128 * c : 128 * c + 128, at]
                    l_ref[128 * c : 128 * c + 128, at] = turned


def invert(place_ref, level, leaf, out_ref):
    for t in range(FB):
        out_ref[t] = -1
    for a in range(UB):
        out_ref[place_ref[level, leaf, a]] = a


def assemble_kernel(
    info_ref, place_ref, own_ref, other_ref, sep_own_ref, sep_other_ref,
    pivot_ref, front_ref, upper_ref, moved_ref, send_ref,
    child_ref, sep_ref, left_ref, right_ref, next_ref, from_left_ref, from_right_ref,
):
    leaf, core = info_ref[0], info_ref[2]
    head = leaf - core
    invert(place_ref, 0, head, left_ref)
    invert(place_ref, 0, head + 1, right_ref)
    invert(place_ref, 1, head, next_ref)
    for t in range(FB):
        source = next_ref[t]
        at = jnp.maximum(source, 0) + SB
        from_left_ref[t] = jnp.where(source >= 0, left_ref[at], -1)
        from_right_ref[t] = jnp.where(source >= 0, right_ref[at], -1)

    @pl.when(core == 0)
    def _():
        child_ref[0] = own_ref[...]
        child_ref[1] = other_ref[...]
        sep_ref[...] = sep_own_ref[...]

    @pl.when(core == 1)
    def _():
        child_ref[0] = other_ref[...]
        child_ref[1] = own_ref[...]
        sep_ref[...] = sep_other_ref[...]

    def part(which, row, col):
        at = pl.multiple_of(jnp.maximum(col, 0) * 128, 128)
        value = child_ref[which, jnp.maximum(row, 0), :, pl.ds(at, 128)]
        return jnp.where((row >= 0) & (col >= 0), value, 0.0)

    def pivot_row(t, carry):
        row = left_ref[t]
        for c in range(SB):
            at = slice(128 * c, 128 * c + 128)
            pivot_ref[t, :, at] = part(0, row, left_ref[c]) + sep_ref[0, t, :, at]
        return carry

    lax.fori_loop(0, FB, pivot_row, 0)
    for i, (a, b) in enumerate(UPPER):
        upper_ref[i] = pivot_ref[a, :, 128 * b : 128 * b + 128]

    def front_row(t, carry):
        row_left, row_right = from_left_ref[t], from_right_ref[t]
        for c in range(FB):
            value = part(0, row_left, from_left_ref[c]) + part(1, row_right, from_right_ref[c])
            at = slice(128 * c, 128 * c + 128)
            if c < SB:
                value = value + sep_ref[1, t, :, at]
            front_ref[t, :, at] = value
        source = next_ref[t]
        moved = jnp.where(source >= 0, pivot_ref[jnp.maximum(source, 0) + SB], 0.0)
        moved_ref[t] = moved
        send_ref[t] = jnp.where(core == 0, moved, front_ref[t, :, :S])
        return carry

    lax.fori_loop(0, FB, front_row, 0)


def first_kernel(
    info_ref, all_upper_ref, pivot_ref, moved_ref,
    inv_ref, factor_ref, weight_ref,
    m_ref, l_ref, u_ref,
):
    for p in range(16):
        for i, (a, b) in enumerate(UPPER):
            row = 128 * a + ROWS * p
            m_ref[row : row + ROWS, 128 * b : 128 * b + 128] = all_upper_ref[p, i]
    factorize(m_ref, l_ref, inv_ref, u_ref)
    panel = info_ref[1]
    heads = info_ref[2] == 0
    inverse = inv_ref[...]
    for a in range(SB):
        row = pl.multiple_of(128 * a + ROWS * panel, ROWS)
        factor_ref[a] = jnp.where(heads, l_ref[pl.ds(row, ROWS), :], 0.0)
    below = nt(pivot_ref[SB:].reshape(UB * ROWS, S), inverse).reshape(UB, ROWS, S)
    factor_ref[SB:] = jnp.where(heads, below, 0.0)
    weight_ref[...] = nn(nt(moved_ref[SB:].reshape(UB * ROWS, S), inverse), inverse)


def fetch(info_ref, all_ref, part, first, count, out_ref, sems, slot):
    copies = []
    for y in range(8):
        for other in range(2):
            side = info_ref[3] if other == 0 else 1 - info_ref[3]
            row = pl.multiple_of((2 * y + side) * ROWS, ROWS)
            copies.append(
                pltpu.make_async_copy(
                    all_ref.at[8 * part + y, other, pl.ds(first, count)],
                    out_ref.at[:, pl.ds(row, ROWS), :],
                    sems.at[slot, 2 * y + other],
                )
            )
    for copy in copies:
        copy.start()
    return copies


def update_kernel(info_ref, all_ref, front_ref, weight_ref, pivot_ref, trail_ref, x_ref, sems):
    for copy in fetch(info_ref, all_ref, 0, 0, FB, x_ref, sems, 0):
        copy.wait()
    weight = weight_ref[...]
    for t in range(FB):
        at = slice(128 * t, 128 * t + 128)
        old = front_ref[SB:, :, at].reshape(UB * ROWS, 128)
        value = old - nt(weight, x_ref[t])
        if t < SB:
            pivot_ref[:, at] = value
        else:
            trail_ref[:, 128 * (t - SB) : 128 * (t - SB) + 128] = value


def second_kernel(
    info_ref, all_ref, inv_before_ref,
    inv_ref, strip_ref, cross_ref,
    x_ref, p_ref, m_ref, l_ref, u_ref, sems,
):
    copies = fetch(info_ref, all_ref, 0, 0, SB, x_ref, sems, 0)
    copies += fetch(info_ref, all_ref, 1, 0, SB, p_ref, sems, 1)
    for copy in copies:
        copy.wait()
    cross = nt(x_ref[...].reshape(S, S), inv_before_ref[...])
    cross_ref[...] = cross
    m_ref[...] = p_ref[...].reshape(S, S) - nt(cross, cross)
    factorize(m_ref, l_ref, inv_ref, u_ref)
    panel = info_ref[1]
    for a in range(SB):
        row = pl.multiple_of(128 * a + ROWS * panel, ROWS)
        strip_ref[a] = l_ref[pl.ds(row, ROWS), :]


def last_kernel(
    info_ref, all_ref, inv_before_ref, cross_ref, inv_ref, strip_ref, pivot_ref,
    trail_ref, sibling_ref, factor_ref,
    factors_ref, top_ref,
    x_ref, p_ref, sems,
):
    copies = fetch(info_ref, all_ref, 0, SB, UB, x_ref, sems, 0)
    copies += fetch(info_ref, all_ref, 1, SB, UB, p_ref, sems, 1)
    heads = info_ref[0] % 4 == 0
    factors_ref[0, 0] = factor_ref[...]
    factors_ref[1, 0, :SB] = jnp.where(heads, strip_ref[...], 0.0)
    inverse = inv_ref[...]
    below = nt(pivot_ref[...], inverse)
    factors_ref[1, 0, SB:] = jnp.where(heads, below, 0.0).reshape(UB, ROWS, S)
    weight = nn(below, inverse)
    mixed = nn(nn(weight, cross_ref[...]), inv_before_ref[...])
    for copy in copies:
        copy.wait()
    for t in range(UB):
        at = slice(128 * t, 128 * t + 128)
        value = trail_ref[:, at] + sibling_ref[:, at]
        value = value - nt(weight, p_ref[t]) + nt(mixed, x_ref[t])
        top_ref[0, :, :, at] = jnp.where(heads, value, 0.0).reshape(UB, ROWS, 128)


VM = pl.BlockSpec(memory_space=pltpu.VMEM)
SM = pl.BlockSpec(memory_space=pltpu.SMEM)
HBM = pl.BlockSpec(memory_space=pl.ANY)


def f32(*shape):
    return jax.ShapeDtypeStruct(shape, jnp.float32)


def call(kernel, ins, outs, scratch, name):
    return pl.pallas_call(
        kernel,
        in_specs=ins,
        out_specs=[VM] * len(outs),
        out_shape=outs,
        scratch_shapes=scratch,
        compiler_params=pltpu.CompilerParams(vmem_limit_bytes=VMEM_LIMIT),
        name=name,
    )


def square():
    return pltpu.VMEM((S, S), jnp.float32)


def body(child_update, separator_columns, placement):
    leaf = lax.axis_index(LEAF)
    panel = lax.axis_index(PANEL)
    core = lax.axis_index("core")
    xhi = lax.axis_index("xhi")
    info = jnp.stack([leaf, panel, core, xhi]).astype(jnp.int32)
    own = child_update[0]
    sep = separator_columns[:, 0]
    swap = [(0, 1), (1, 0)]
    other = lax.ppermute(own, "core", swap)
    sep_other = lax.ppermute(sep, "core", swap)
    pivot, front, upper, moved, send = call(
        assemble_kernel,
        [SM, SM, VM, VM, VM, VM],
        [f32(FB, ROWS, S), f32(FB, ROWS, F), f32(len(UPPER), ROWS, 128), f32(FB, ROWS, S), f32(FB, ROWS, S)],
        [pltpu.VMEM((2, UB, ROWS, U), jnp.float32), pltpu.VMEM((2, FB, ROWS, S), jnp.float32)]
        + [pltpu.SMEM((FB,), jnp.int32)] * 5,
        "assemble",
    )(info, placement, own, other, sep, sep_other)
    across = lax.ppermute(send, "xhi", swap)
    gathered = lax.all_gather(jnp.stack([send, across]), ("core", "y"), axis=0, tiled=False)
    copies = jnp.broadcast_to(upper[None], (16,) + upper.shape)
    copies, _ = lax.optimization_barrier((copies, across))
    all_upper = lax.all_to_all(copies, PANEL, 0, 0, tiled=True)
    inv0, factor0, weight = call(
        first_kernel,
        [SM, VM, VM, VM],
        [f32(S, S), f32(FB, ROWS, S), f32(UB * ROWS, S)],
        [square(), square(), pltpu.VMEM((128, S), jnp.float32)],
        "first",
    )(info, all_upper, pivot, moved)
    gathered = gathered.reshape(16, 2, FB, ROWS, S)
    below, trail = call(
        update_kernel,
        [SM, HBM, VM, VM],
        [f32(UB * ROWS, S), f32(UB * ROWS, U)],
        [pltpu.VMEM((FB, 128, S), jnp.float32), pltpu.SemaphoreType.DMA((1, 16))],
        "update",
    )(info, gathered, front, weight)
    heads = [(first + 2, first) for first in range(0, 32, 4)]
    sibling = lax.ppermute(trail, LEAF, heads)
    inv1, strip, cross = call(
        second_kernel,
        [SM, HBM, VM],
        [f32(S, S), f32(SB, ROWS, S), f32(S, S)],
        [pltpu.VMEM((SB, 128, S), jnp.float32)] * 2
        + [square(), square(), pltpu.VMEM((128, S), jnp.float32), pltpu.SemaphoreType.DMA((2, 16))],
        "second",
    )(info, gathered, inv0)
    return tuple(
        call(
            last_kernel,
            [SM, HBM] + [VM] * 8,
            [f32(2, 1, FB, ROWS, S), f32(1, UB, ROWS, U)],
            [pltpu.VMEM((UB, 128, S), jnp.float32)] * 2 + [pltpu.SemaphoreType.DMA((2, 16))],
            "last",
        )(info, gathered, inv0, cross, inv1, strip, below, trail, sibling, factor0)
    )


def solution(mesh):
    fine = Mesh(mesh.devices.reshape(8, 2, 2, 8, 2), AXES)
    update = P(LEAF, None, PANEL, None)
    columns = P(None, LEAF, None, PANEL, None)
    return jax.shard_map(
        body,
        mesh=fine,
        in_specs=(update, columns, P()),
        out_specs=(columns, update),
        check_vma=False,
    )
```

```python
import jax
import jax.numpy as jnp
from jax import lax
from jax.experimental import pallas as pl
from jax.experimental.pallas import tpu as pltpu
from jax.sharding import Mesh
from jax.sharding import PartitionSpec as P

F = 2048
S = 512
U = 1536
FB = 16
SB = 4
UB = 12
ROWS = 8
SLOTS = 14
BLOCK = 32
HALF = 16
HI = lax.Precision.HIGHEST
AXES = ("z", "xlo", "core", "y", "xhi")
LEAF = ("z", "xlo", "core")
PANEL = ("y", "xhi")
UPPER = [(a, b) for a in range(SB) for b in range(a, SB)]
VMEM_LIMIT = 48 << 20


def nt(a, b):
    return lax.dot_general(
        a, b, (((1,), (1,)), ((), ())), precision=HI, preferred_element_type=jnp.float32
    )


def nn(a, b):
    return jnp.dot(a, b, precision=HI, preferred_element_type=jnp.float32)


def spread_row(tile, row):
    return jnp.broadcast_to(tile[row : row + 1, :], tile.shape)


def split3(x):
    high = x.astype(jnp.bfloat16)
    rest = x - high.astype(jnp.float32)
    mid = rest.astype(jnp.bfloat16)
    low = (rest - mid.astype(jnp.float32)).astype(jnp.bfloat16)
    return high, mid, low


def factor_block(m_ref, start):
    tile, lo = start // 128, start % 128
    groups, cols = BLOCK // 8, S // 128
    lane = lax.broadcasted_iota(jnp.int32, (8, 128), 1)
    sub = lax.broadcasted_iota(jnp.int32, (8, 128), 0)
    rows = [
        [m_ref[start + 8 * g : start + 8 * g + 8, 128 * c : 128 * c + 128] for c in range(cols)]
        for g in range(groups)
    ]
    diag = [rows[g][tile] for g in range(groups)]
    inside = (lane >= lo) & (lane < lo + BLOCK)
    for g in range(groups):
        unit = jnp.where(lane == sub + (lo + 8 * g), 1.0, 0.0)
        rows[g][tile] = jnp.where(inside, unit, diag[g])
    factor = [jnp.zeros((8, 128), jnp.float32) for _ in range(groups)]
    for first in range(0, BLOCK, HALF):
        spread = {
            k: {
                g: jnp.broadcast_to(diag[g][:, lo + k : lo + k + 1], (8, 128))
                for g in range(k // 8, groups)
            }
            for k in range(first, first + HALF)
        }
        last = first + HALF == BLOCK
        for j in range(first, first + HALF):
            gj, s = j // 8, j % 8
            inv = lax.rsqrt(spread_row(spread[j][gj], s))
            col = {g: spread[j][g] * inv for g in range(gj, groups)}
            for k in range(j + 1, first + HALF):
                w = spread_row(col[k // 8], k % 8)
                for g in range(k // 8, groups):
                    spread[k][g] = spread[k][g] - col[g] * w
            below = jnp.where(sub > s, col[gj], 0.0)
            factor[gj] = jnp.where((lane == lo + j) & (sub >= s), col[gj], factor[gj])
            for g in range(gj + 1, groups):
                factor[g] = jnp.where(lane == lo + j, col[g], factor[g])
            for c in range(cols):
                u = spread_row(rows[gj][c], s) * inv
                rows[gj][c] = jnp.where(sub == s, u, rows[gj][c] - below * u)
                for g in range(gj + 1, groups):
                    rows[g][c] = rows[g][c] - col[g] * u
            if not last:
                u = spread_row(diag[gj], s) * inv
                diag[gj] = jnp.where(sub == s, u, diag[gj] - below * u)
                for g in range(gj + 1, groups):
                    diag[g] = diag[g] - col[g] * u
    joined = [jnp.concatenate([rows[g][c] for g in range(groups)], 0) for c in range(cols)]
    return joined, jnp.concatenate(factor, 0)


def factorize(m_ref, l_ref, inv_ref, u_ref):
    cols = S // 128
    lane = lax.broadcasted_iota(jnp.int32, (BLOCK, 128), 1)
    for start in range(0, S, BLOCK):
        end, tile, lo = start + BLOCK, start // 128, start % 128
        rows, diag = factor_block(m_ref, start)
        for c in range(cols):
            if c < tile:
                value = rows[c]
            elif c == tile:
                value = jnp.where(lane < lo + BLOCK, rows[c], 0.0)
            else:
                value = jnp.zeros_like(rows[c])
            inv_ref[start:end, 128 * c : 128 * c + 128] = value
        upper = [jnp.where(lane >= lo + BLOCK, rows[tile], 0.0)] + rows[tile + 1 :]
        for i, value in enumerate(upper):
            c = tile + i
            u_ref[lo : lo + BLOCK, 128 * c : 128 * c + 128] = value
        l_ref[start:end, 128 * tile : 128 * tile + 128] = diag
        if end < S:
            skip = end // 128 - tile
            left = split3(jnp.concatenate(upper[skip:], 1))
            right = split3(jnp.concatenate(rows, 1))
            pairs = ((0, 0), (0, 1), (1, 0), (1, 1), (0, 2), (2, 0))
            update = lax.dot_general(
                jnp.concatenate([left[a] for a, _ in pairs], 0),
                jnp.concatenate([right[b] for _, b in pairs], 0),
                (((0,), (0,)), ((), ())),
                preferred_element_type=jnp.float32,
            )
            offset = end % 128 if skip == 0 else 0
            for c in range(cols):
                value = m_ref[end:S, 128 * c : 128 * c + 128]
                if c == tile:
                    at = lax.broadcasted_iota(jnp.int32, value.shape, 1)
                    value = jnp.where((at >= lo) & (at < lo + BLOCK), 0.0, value)
                m_ref[end:S, 128 * c : 128 * c + 128] = (
                    value - update[offset:, 128 * c : 128 * c + 128]
                )
        if end % 128 == 0:
            at = slice(128 * tile, 128 * tile + 128)
            for c in range(cols):
                if c < tile:
                    l_ref[128 * c : 128 * c + 128, at] = jnp.zeros((128, 128), jnp.float32)
                else:
                    turned = u_ref[:, 128 * c : 128 * c + 128].T
                    if c == tile:
                        turned = turned + l_ref[128 * c : 128 * c + 128, at]
                    l_ref[128 * c : 128 * c + 128, at] = turned


def invert(place_ref, level, leaf, out_ref):
    for t in range(FB):
        out_ref[t] = -1
    for a in range(UB):
        out_ref[place_ref[level, leaf, a]] = a


def assemble_kernel(
    info_ref, place_ref, own_ref, other_ref, sep_own_ref, sep_other_ref,
    pivot_ref, front_ref, upper_ref, send_ref, next_ref,
    child_ref, sep_ref, left_ref, right_ref, from_left_ref, from_right_ref, sems,
):
    leaf, core = info_ref[0], info_ref[2]
    copies = [
        pltpu.make_async_copy(own_ref.at[0], child_ref.at[core], sems.at[0]),
        pltpu.make_async_copy(other_ref, child_ref.at[1 - core], sems.at[1]),
        pltpu.make_async_copy(sep_own_ref.at[:, 0], sep_ref.at[core], sems.at[2]),
        pltpu.make_async_copy(sep_other_ref, sep_ref.at[1 - core], sems.at[3]),
    ]
    for copy in copies:
        copy.start()
    head = leaf - core
    invert(place_ref, 0, head, left_ref)
    invert(place_ref, 0, head + 1, right_ref)
    invert(place_ref, 1, head, next_ref)
    for t in range(FB):
        source = next_ref[t]
        at = jnp.maximum(source, 0) + SB
        from_left_ref[t] = jnp.where(source >= 0, left_ref[at], -1)
        from_right_ref[t] = jnp.where(source >= 0, right_ref[at], -1)
    for copy in copies:
        copy.wait()

    def part(which, row, col):
        at = pl.multiple_of(jnp.maximum(col, 0) * 128, 128)
        value = child_ref[which, jnp.maximum(row, 0), :, pl.ds(at, 128)]
        return jnp.where((row >= 0) & (col >= 0), value, 0.0)

    def pivot_row(t, carry):
        row = left_ref[t]
        for c in range(SB):
            at = slice(128 * c, 128 * c + 128)
            pivot_ref[t, :, at] = part(0, row, left_ref[c]) + sep_ref[0, 0, t, :, at]
        return carry

    lax.fori_loop(0, FB, pivot_row, 0)
    for i, (a, b) in enumerate(UPPER):
        upper_ref[i] = pivot_ref[a, :, 128 * b : 128 * b + 128]

    def front_row(t, carry):
        row_left, row_right = from_left_ref[t], from_right_ref[t]
        for c in range(FB):
            value = part(0, row_left, from_left_ref[c]) + part(1, row_right, from_right_ref[c])
            at = slice(128 * c, 128 * c + 128)
            if c < SB:
                value = value + sep_ref[0, 1, t, :, at]
            front_ref[t, :, at] = value
        return carry

    lax.fori_loop(0, FB, front_row, 0)
    for i in range(UB):
        send_ref[i] = jnp.where(core == 0, pivot_ref[SB + i], front_ref[i, :, :S])
    for i in range(UB, SLOTS):
        send_ref[i] = jnp.where(core == 0, front_ref[i + 2, :, :S], front_ref[i, :, :S])


def first_kernel(
    info_ref, all_upper_ref, pivot_ref,
    inv_ref, factor_ref, weight_ref,
    m_ref, l_ref, u_ref,
):
    for p in range(16):
        for i, (a, b) in enumerate(UPPER):
            row = 128 * a + ROWS * p
            m_ref[row : row + ROWS, 128 * b : 128 * b + 128] = all_upper_ref[p, i]
    factorize(m_ref, l_ref, inv_ref, u_ref)
    panel = info_ref[1]
    heads = info_ref[2] == 0
    inverse = inv_ref[...]
    for a in range(SB):
        row = pl.multiple_of(128 * a + ROWS * panel, ROWS)
        factor_ref[a] = jnp.where(heads, l_ref[pl.ds(row, ROWS), :], 0.0)
    below = nt(pivot_ref[SB:].reshape(UB * ROWS, S), inverse)
    factor_ref[SB:] = jnp.where(heads, below.reshape(UB, ROWS, S), 0.0)
    weight_ref[...] = nn(below, inverse).reshape(UB, ROWS, S)


def fetch(all_ref, out_ref, sems):
    copies = [
        pltpu.make_async_copy(all_ref.at[i], out_ref.at[i], sems.at[i])
        for i in range(out_ref.shape[0])
    ]
    for copy in copies:
        copy.start()
    return copies


def strips(ref, base, slot, side):
    sides = (side, 1 - side)
    return jnp.concatenate([ref[base + y, sides[x], slot] for y in range(8) for x in range(2)], 0)


def update_kernel(
    info_ref, next_ref, all_ref, front_ref, weight_ref,
    pivot_ref, trail_ref, cross_ref,
    all_vmem, w_ref, sems,
):
    copies = fetch(all_ref, all_vmem, sems)
    for t in range(UB):
        source = next_ref[SB + t]
        moved = weight_ref[jnp.maximum(source, 0)]
        w_ref[ROWS * t : ROWS * t + ROWS, :] = jnp.where(source >= 0, moved, 0.0)
    weight = w_ref[...]
    for copy in copies:
        copy.wait()
    side = info_ref[3]
    for t in range(FB):
        source = next_ref[t]
        x = strips(all_vmem, 0, jnp.maximum(source, 0), side)
        if t < SB:
            cross_ref[t] = jnp.where(source >= 0, x, 0.0)
        at = slice(128 * t, 128 * t + 128)
        value = front_ref[SB:, :, at].reshape(UB * ROWS, 128)
        value = value - jnp.where(source >= 0, nt(x, weight).T, 0.0)
        if t < SB:
            pivot_ref[:, at] = value
        else:
            trail_ref[:, 128 * (t - SB) : 128 * (t - SB) + 128] = value


def second_kernel(
    info_ref, all_ref, x_ref, inv_before_ref,
    inv_ref, strip_ref, cross_ref,
    p_ref, m_ref, l_ref, u_ref, sems,
):
    copies = [
        pltpu.make_async_copy(all_ref.at[8 + y, :, pl.ds(0, SB)], p_ref.at[y], sems.at[y])
        for y in range(8)
    ]
    for copy in copies:
        copy.start()
    cross = nt(x_ref[...].reshape(S, S), inv_before_ref[...])
    cross_ref[...] = cross
    for copy in copies:
        copy.wait()
    product = nt(cross, cross)
    for a in range(SB):
        at = slice(128 * a, 128 * a + 128)
        m_ref[at, :] = strips(p_ref, 0, a, info_ref[3]) - product[at, :]
    factorize(m_ref, l_ref, inv_ref, u_ref)
    panel = info_ref[1]
    for a in range(SB):
        row = pl.multiple_of(128 * a + ROWS * panel, ROWS)
        strip_ref[a] = l_ref[pl.ds(row, ROWS), :]


def last_kernel(
    info_ref, next_ref, all_ref, inv_before_ref, cross_ref, inv_ref, strip_ref, pivot_ref,
    trail_ref, sibling_ref, factor_ref,
    factors_ref, top_ref,
    all_vmem, sems,
):
    copies = fetch(all_ref, all_vmem, sems)
    heads = info_ref[0] % 4 == 0
    factors_ref[0, 0] = factor_ref[...]
    factors_ref[1, 0, :SB] = jnp.where(heads, strip_ref[...], 0.0)
    inverse = inv_ref[...]
    below = nt(pivot_ref[...], inverse)
    factors_ref[1, 0, SB:] = jnp.where(heads, below, 0.0).reshape(UB, ROWS, S)
    weight = nn(below, inverse)
    mixed = nn(nn(weight, cross_ref[...]), inv_before_ref[...])
    for copy in copies:
        copy.wait()
    side = info_ref[3]
    for t in range(UB):
        at = slice(128 * t, 128 * t + 128)
        source = next_ref[SB + t]
        block = SB + t
        p = strips(all_vmem, 8, block, side) if block < SLOTS else strips(all_vmem, 0, block - 2, side)
        x = strips(all_vmem, 0, jnp.maximum(source, 0), side)
        value = trail_ref[:, at] + sibling_ref[:, at]
        value = value - nt(p, weight).T + jnp.where(source >= 0, nt(x, mixed).T, 0.0)
        top_ref[0, :, :, at] = jnp.where(heads, value, 0.0).reshape(UB, ROWS, 128)


VM = pl.BlockSpec(memory_space=pltpu.VMEM)
SM = pl.BlockSpec(memory_space=pltpu.SMEM)
HBM = pl.BlockSpec(memory_space=pl.ANY)


def f32(*shape):
    return jax.ShapeDtypeStruct(shape, jnp.float32)


def call(kernel, ins, outs, scratch, name):
    return pl.pallas_call(
        kernel,
        in_specs=ins,
        out_specs=[SM if out.dtype == jnp.int32 else VM for out in outs],
        out_shape=outs,
        scratch_shapes=scratch,
        compiler_params=pltpu.CompilerParams(vmem_limit_bytes=VMEM_LIMIT),
        name=name,
    )


def vmem(*shape):
    return pltpu.VMEM(shape, jnp.float32)


def body(child_update, separator_columns, placement):
    leaf = lax.axis_index(LEAF)
    panel = lax.axis_index(PANEL)
    core = lax.axis_index("core")
    xhi = lax.axis_index("xhi")
    info = jnp.stack([leaf, panel, core, xhi]).astype(jnp.int32)
    swap = [(0, 1), (1, 0)]
    other = lax.ppermute(child_update[0], "core", swap)
    sep_other = lax.ppermute(separator_columns[:, 0], "core", swap)
    pivot, front, upper, send, following = call(
        assemble_kernel,
        [SM, SM, HBM, HBM, HBM, HBM],
        [f32(FB, ROWS, S), f32(FB, ROWS, F), f32(len(UPPER), ROWS, 128), f32(SLOTS, ROWS, S),
         jax.ShapeDtypeStruct((FB,), jnp.int32)],
        [vmem(2, UB, ROWS, U), vmem(2, 2, FB, ROWS, S)]
        + [pltpu.SMEM((FB,), jnp.int32)] * 4 + [pltpu.SemaphoreType.DMA((4,))],
        "assemble",
    )(info, placement, child_update, other, separator_columns, sep_other)
    across = lax.ppermute(send, "xhi", swap)
    gathered = lax.all_gather(jnp.stack([send, across]), ("core", "y"), axis=0, tiled=False)
    gathered = gathered.reshape(16, 2, SLOTS, ROWS, S)
    copies = jnp.broadcast_to(upper[None], (16,) + upper.shape)
    copies, _ = lax.optimization_barrier((copies, across))
    all_upper = lax.all_to_all(copies, PANEL, 0, 0, tiled=True)
    inv0, factor0, weight = call(
        first_kernel,
        [SM, VM, VM],
        [f32(S, S), f32(FB, ROWS, S), f32(UB, ROWS, S)],
        [vmem(S, S), vmem(S, S), vmem(128, S)],
        "first",
    )(info, all_upper, pivot)
    below, trail, moved = call(
        update_kernel,
        [SM, SM, HBM, VM, VM],
        [f32(UB * ROWS, S), f32(UB * ROWS, U), f32(SB, 128, S)],
        [vmem(8, 2, SLOTS, ROWS, S), vmem(UB * ROWS, S), pltpu.SemaphoreType.DMA((8,))],
        "update",
    )(info, following, gathered, front, weight)
    heads = [(first + 2, first) for first in range(0, 32, 4)]
    sibling = lax.ppermute(trail, LEAF, heads)
    inv1, strip, cross = call(
        second_kernel,
        [SM, HBM, VM, VM],
        [f32(S, S), f32(SB, ROWS, S), f32(S, S)],
        [vmem(8, 2, SB, ROWS, S), vmem(S, S), vmem(S, S), vmem(128, S), pltpu.SemaphoreType.DMA((8,))],
        "second",
    )(info, gathered, moved, inv0)
    return tuple(
        call(
            last_kernel,
            [SM, SM, HBM] + [VM] * 8,
            [f32(2, 1, FB, ROWS, S), f32(1, UB, ROWS, U)],
            [vmem(16, 2, SLOTS, ROWS, S), pltpu.SemaphoreType.DMA((16,))],
            "last",
        )(info, following, gathered, inv0, cross, inv1, strip, below, trail, sibling, factor0)
    )


def solution(mesh):
    fine = Mesh(mesh.devices.reshape(8, 2, 2, 8, 2), AXES)
    update = P(LEAF, None, PANEL, None)
    columns = P(None, LEAF, None, PANEL, None)
    return jax.shard_map(
        body,
        mesh=fine,
        in_specs=(update, columns, P()),
        out_specs=(columns, update),
        check_vma=False,
    )
```

```python
import jax
import jax.numpy as jnp
from jax import lax
from jax.experimental import pallas as pl
from jax.experimental.pallas import tpu as pltpu
from jax.sharding import Mesh
from jax.sharding import PartitionSpec as P

F = 2048
S = 512
U = 1536
FB = 16
SB = 4
UB = 12
ROWS = 8
SLOTS = 14
BLOCK = 32
HALF = 16
HI = lax.Precision.HIGHEST
AXES = ("z", "xlo", "core", "y", "xhi")
LEAF = ("z", "xlo", "core")
PANEL = ("y", "xhi")
UPPER = [(a, b) for a in range(SB) for b in range(a, SB)]
VMEM_LIMIT = 20 << 20


def nt(a, b):
    return lax.dot_general(
        a, b, (((1,), (1,)), ((), ())), precision=HI, preferred_element_type=jnp.float32
    )


def nn(a, b):
    return jnp.dot(a, b, precision=HI, preferred_element_type=jnp.float32)


def spread_row(tile, row):
    return jnp.broadcast_to(tile[row : row + 1, :], tile.shape)


def split3(x):
    high = x.astype(jnp.bfloat16)
    rest = x - high.astype(jnp.float32)
    mid = rest.astype(jnp.bfloat16)
    low = (rest - mid.astype(jnp.float32)).astype(jnp.bfloat16)
    return high, mid, low


def factor_block(m_ref, start):
    tile, lo = start // 128, start % 128
    groups, cols = BLOCK // 8, S // 128
    lane = lax.broadcasted_iota(jnp.int32, (8, 128), 1)
    sub = lax.broadcasted_iota(jnp.int32, (8, 128), 0)
    rows = [
        [m_ref[start + 8 * g : start + 8 * g + 8, 128 * c : 128 * c + 128] for c in range(cols)]
        for g in range(groups)
    ]
    diag = [rows[g][tile] for g in range(groups)]
    inside = (lane >= lo) & (lane < lo + BLOCK)
    for g in range(groups):
        unit = jnp.where(lane == sub + (lo + 8 * g), 1.0, 0.0)
        rows[g][tile] = jnp.where(inside, unit, diag[g])
    factor = [jnp.zeros((8, 128), jnp.float32) for _ in range(groups)]
    for first in range(0, BLOCK, HALF):
        spread = {
            k: {
                g: jnp.broadcast_to(diag[g][:, lo + k : lo + k + 1], (8, 128))
                for g in range(k // 8, groups)
            }
            for k in range(first, first + HALF)
        }
        last = first + HALF == BLOCK
        for j in range(first, first + HALF):
            gj, s = j // 8, j % 8
            inv = lax.rsqrt(spread_row(spread[j][gj], s))
            col = {g: spread[j][g] * inv for g in range(gj, groups)}
            for k in range(j + 1, first + HALF):
                w = spread_row(col[k // 8], k % 8)
                for g in range(k // 8, groups):
                    spread[k][g] = spread[k][g] - col[g] * w
            below = jnp.where(sub > s, col[gj], 0.0)
            factor[gj] = jnp.where((lane == lo + j) & (sub >= s), col[gj], factor[gj])
            for g in range(gj + 1, groups):
                factor[g] = jnp.where(lane == lo + j, col[g], factor[g])
            for c in range(cols):
                u = spread_row(rows[gj][c], s) * inv
                rows[gj][c] = jnp.where(sub == s, u, rows[gj][c] - below * u)
                for g in range(gj + 1, groups):
                    rows[g][c] = rows[g][c] - col[g] * u
            if not last:
                u = spread_row(diag[gj], s) * inv
                diag[gj] = jnp.where(sub == s, u, diag[gj] - below * u)
                for g in range(gj + 1, groups):
                    diag[g] = diag[g] - col[g] * u
    joined = [jnp.concatenate([rows[g][c] for g in range(groups)], 0) for c in range(cols)]
    return joined, jnp.concatenate(factor, 0)


def factorize(m_ref, l_ref, inv_ref, u_ref):
    cols = S // 128
    lane = lax.broadcasted_iota(jnp.int32, (BLOCK, 128), 1)
    for start in range(0, S, BLOCK):
        end, tile, lo = start + BLOCK, start // 128, start % 128
        rows, diag = factor_block(m_ref, start)
        for c in range(cols):
            if c < tile:
                value = rows[c]
            elif c == tile:
                value = jnp.where(lane < lo + BLOCK, rows[c], 0.0)
            else:
                value = jnp.zeros_like(rows[c])
            inv_ref[start:end, 128 * c : 128 * c + 128] = value
        upper = [jnp.where(lane >= lo + BLOCK, rows[tile], 0.0)] + rows[tile + 1 :]
        for i, value in enumerate(upper):
            c = tile + i
            u_ref[lo : lo + BLOCK, 128 * c : 128 * c + 128] = value
        l_ref[start:end, 128 * tile : 128 * tile + 128] = diag
        if end < S:
            skip = end // 128 - tile
            left = split3(jnp.concatenate(upper[skip:], 1))
            right = split3(jnp.concatenate(rows, 1))
            pairs = ((0, 0), (0, 1), (1, 0), (1, 1), (0, 2), (2, 0))
            update = lax.dot_general(
                jnp.concatenate([left[a] for a, _ in pairs], 0),
                jnp.concatenate([right[b] for _, b in pairs], 0),
                (((0,), (0,)), ((), ())),
                preferred_element_type=jnp.float32,
            )
            offset = end % 128 if skip == 0 else 0
            for c in range(cols):
                value = m_ref[end:S, 128 * c : 128 * c + 128]
                if c == tile:
                    at = lax.broadcasted_iota(jnp.int32, value.shape, 1)
                    value = jnp.where((at >= lo) & (at < lo + BLOCK), 0.0, value)
                m_ref[end:S, 128 * c : 128 * c + 128] = (
                    value - update[offset:, 128 * c : 128 * c + 128]
                )
        if end % 128 == 0:
            at = slice(128 * tile, 128 * tile + 128)
            for c in range(cols):
                if c < tile:
                    l_ref[128 * c : 128 * c + 128, at] = jnp.zeros((128, 128), jnp.float32)
                else:
                    turned = u_ref[:, 128 * c : 128 * c + 128].T
                    if c == tile:
                        turned = turned + l_ref[128 * c : 128 * c + 128, at]
                    l_ref[128 * c : 128 * c + 128, at] = turned


def invert(place_ref, level, leaf, out_ref):
    for t in range(FB):
        out_ref[t] = -1
    for a in range(UB):
        out_ref[place_ref[level, leaf, a]] = a


def assemble_kernel(
    info_ref, place_ref, own_ref, other_ref, sep_own_ref, sep_other_ref,
    pivot_ref, front_ref, upper_ref, send_ref, next_ref,
    child_ref, sep_ref, left_ref, right_ref, from_left_ref, from_right_ref, sems,
):
    leaf, core = info_ref[0], info_ref[2]
    copies = [
        pltpu.make_async_copy(own_ref.at[0], child_ref.at[core], sems.at[0]),
        pltpu.make_async_copy(other_ref, child_ref.at[1 - core], sems.at[1]),
        pltpu.make_async_copy(sep_own_ref.at[:, 0], sep_ref.at[core], sems.at[2]),
        pltpu.make_async_copy(sep_other_ref, sep_ref.at[1 - core], sems.at[3]),
    ]
    for copy in copies:
        copy.start()
    head = leaf - core
    invert(place_ref, 0, head, left_ref)
    invert(place_ref, 0, head + 1, right_ref)
    invert(place_ref, 1, head, next_ref)
    for t in range(FB):
        source = next_ref[t]
        at = jnp.maximum(source, 0) + SB
        from_left_ref[t] = jnp.where(source >= 0, left_ref[at], -1)
        from_right_ref[t] = jnp.where(source >= 0, right_ref[at], -1)
    for copy in copies:
        copy.wait()

    def part(which, row, col):
        at = pl.multiple_of(jnp.maximum(col, 0) * 128, 128)
        value = child_ref[which, jnp.maximum(row, 0), :, pl.ds(at, 128)]
        return jnp.where((row >= 0) & (col >= 0), value, 0.0)

    def pivot_row(t, carry):
        row = left_ref[t]
        for c in range(SB):
            at = slice(128 * c, 128 * c + 128)
            pivot_ref[t, :, at] = part(0, row, left_ref[c]) + sep_ref[0, 0, t, :, at]
        return carry

    lax.fori_loop(0, FB, pivot_row, 0)
    for i, (a, b) in enumerate(UPPER):
        upper_ref[i] = pivot_ref[a, :, 128 * b : 128 * b + 128]

    def front_row(t, carry):
        row_left, row_right = from_left_ref[t], from_right_ref[t]
        for c in range(FB):
            value = part(0, row_left, from_left_ref[c]) + part(1, row_right, from_right_ref[c])
            at = slice(128 * c, 128 * c + 128)
            if c < SB:
                value = value + sep_ref[0, 1, t, :, at]
            front_ref[t, :, at] = value
        return carry

    lax.fori_loop(0, FB, front_row, 0)
    for i in range(UB):
        send_ref[i] = jnp.where(core == 0, pivot_ref[SB + i], front_ref[i, :, :S])
    for i in range(UB, SLOTS):
        send_ref[i] = jnp.where(core == 0, front_ref[i + 2, :, :S], front_ref[i, :, :S])


def first_kernel(
    info_ref, all_upper_ref, pivot_ref,
    inv_ref, factor_ref, weight_ref,
    m_ref, l_ref, u_ref,
):
    for p in range(16):
        for i, (a, b) in enumerate(UPPER):
            row = 128 * a + ROWS * p
            m_ref[row : row + ROWS, 128 * b : 128 * b + 128] = all_upper_ref[p, i]
    factorize(m_ref, l_ref, inv_ref, u_ref)
    panel = info_ref[1]
    heads = info_ref[2] == 0
    inverse = inv_ref[...]
    for a in range(SB):
        row = pl.multiple_of(128 * a + ROWS * panel, ROWS)
        factor_ref[a] = jnp.where(heads, l_ref[pl.ds(row, ROWS), :], 0.0)
    below = nt(pivot_ref[SB:].reshape(UB * ROWS, S), inverse)
    factor_ref[SB:] = jnp.where(heads, below.reshape(UB, ROWS, S), 0.0)
    weight_ref[...] = nn(below, inverse).reshape(UB, ROWS, S)


def strips(ref, base, slot, side):
    sides = (side, 1 - side)
    return jnp.concatenate([ref[base + y, sides[x], slot] for y in range(8) for x in range(2)], 0)


def second_kernel(
    info_ref, next_ref, all_ref, front_ref, weight_ref, inv_before_ref,
    inv_ref, strip_ref, cross_ref, x_ref, w_ref, trail_ref, kept_ref,
    p_ref, m_ref, l_ref, u_ref, sems,
):
    side = info_ref[3]
    first = []
    for y in range(8):
        first.append(
            pltpu.make_async_copy(all_ref.at[8 + y, :, pl.ds(0, SB)], p_ref.at[y], sems.at[len(first)])
        )
    for t in range(SB):
        source = jnp.maximum(next_ref[t], 0)
        for y in range(8):
            for other in range(2):
                at = 2 * y + (side if other == 0 else 1 - side)
                row = pl.multiple_of(at * ROWS, ROWS)
                first.append(
                    pltpu.make_async_copy(
                        all_ref.at[y, other, source],
                        x_ref.at[t, pl.ds(row, ROWS)],
                        sems.at[len(first)],
                    )
                )
    rest = [
        pltpu.make_async_copy(all_ref.at[i], kept_ref.at[i], sems.at[len(first) + i])
        for i in range(16)
    ]
    for copy in first + rest:
        copy.start()
    for t in range(UB):
        source = next_ref[SB + t]
        moved = weight_ref[jnp.maximum(source, 0)]
        w_ref[ROWS * t : ROWS * t + ROWS, :] = jnp.where(source >= 0, moved, 0.0)
    for copy in first:
        copy.wait()
    heads = (info_ref[0] - info_ref[2]) % 4 == 0

    @pl.when(heads)
    def _():
        for t in range(SB):
            x_ref[t] = jnp.where(next_ref[t] >= 0, x_ref[t], 0.0)
        cross = nt(x_ref[...].reshape(S, S), inv_before_ref[...])
        cross_ref[...] = cross
        product = nt(cross, cross)
        for a in range(SB):
            at = slice(128 * a, 128 * a + 128)
            m_ref[at, :] = strips(p_ref, 0, a, side) - product[at, :]
        factorize(m_ref, l_ref, inv_ref, u_ref)
        for a in range(SB):
            row = pl.multiple_of(128 * a + ROWS * info_ref[1], ROWS)
            strip_ref[a] = l_ref[pl.ds(row, ROWS), :]

    for copy in rest:
        copy.wait()

    @pl.when(jnp.logical_not(heads))
    def _():
        weight = w_ref[...]
        for t in range(UB):
            source = next_ref[SB + t]
            x = strips(kept_ref, 0, jnp.maximum(source, 0), side)
            old = front_ref[SB:, :, S + 128 * t : S + 128 * t + 128].reshape(UB * ROWS, 128)
            product = jnp.where(source >= 0, nt(x, weight).T, 0.0)
            trail_ref[:, 128 * t : 128 * t + 128] = old - product


def last_kernel(
    info_ref, next_ref, kept_ref, front_ref, x_ref, w_ref, inv_before_ref, cross_ref,
    inv_ref, strip_ref, factor_ref,
    factors_ref, part_ref,
):
    side = info_ref[3]
    heads = info_ref[0] % 4 == 0
    factors_ref[0, 0] = factor_ref[...]

    @pl.when(heads)
    def _():
        inverse = inv_ref[...]
        before = w_ref[...]
        pivots = front_ref[SB:, :, :S].reshape(UB * ROWS, S) - nt(before, x_ref[...].reshape(S, S))
        below = nt(pivots, inverse)
        factors_ref[1, 0, :SB] = strip_ref[...]
        factors_ref[1, 0, SB:] = below.reshape(UB, ROWS, S)
        weight = nn(below, inverse)
        mixed = before - nn(nn(weight, cross_ref[...]), inv_before_ref[...])
        for t in range(UB):
            source = next_ref[SB + t]
            block = SB + t
            if block < SLOTS:
                p = strips(kept_ref, 8, block, side)
            else:
                p = strips(kept_ref, 0, block - 2, side)
            x = strips(kept_ref, 0, jnp.maximum(source, 0), side)
            old = front_ref[SB:, :, S + 128 * t : S + 128 * t + 128].reshape(UB * ROWS, 128)
            value = old - nt(p, weight).T - jnp.where(source >= 0, nt(x, mixed).T, 0.0)
            part_ref[:, 128 * t : 128 * t + 128] = value

    @pl.when(jnp.logical_not(heads))
    def _():
        factors_ref[1, 0] = jnp.zeros((FB, ROWS, S), jnp.float32)
        part_ref[...] = jnp.zeros((UB * ROWS, U), jnp.float32)


VM = pl.BlockSpec(memory_space=pltpu.VMEM)
SM = pl.BlockSpec(memory_space=pltpu.SMEM)
HBM = pl.BlockSpec(memory_space=pltpu.HBM)


def f32(*shape):
    return jax.ShapeDtypeStruct(shape, jnp.float32)


def call(kernel, ins, outs, scratch, name):
    return pl.pallas_call(
        kernel,
        in_specs=ins,
        out_specs=[SM if out.dtype == jnp.int32 else VM for out in outs],
        out_shape=outs,
        scratch_shapes=scratch,
        compiler_params=pltpu.CompilerParams(vmem_limit_bytes=VMEM_LIMIT),
        name=name,
    )


def vmem(*shape):
    return pltpu.VMEM(shape, jnp.float32)


def body(child_update, separator_columns, placement):
    leaf = lax.axis_index(LEAF)
    panel = lax.axis_index(PANEL)
    core = lax.axis_index("core")
    xhi = lax.axis_index("xhi")
    info = jnp.stack([leaf, panel, core, xhi]).astype(jnp.int32)
    swap = [(0, 1), (1, 0)]
    other = lax.ppermute(child_update[0], "core", swap)
    sep_other = lax.ppermute(separator_columns[:, 0], "core", swap)
    held = pltpu.with_memory_space_constraint(child_update, pltpu.HBM)
    held_sep = pltpu.with_memory_space_constraint(separator_columns, pltpu.HBM)
    pivot, front, upper, send, following = call(
        assemble_kernel,
        [SM, SM, HBM, HBM, HBM, HBM],
        [f32(FB, ROWS, S), f32(FB, ROWS, F), f32(len(UPPER), ROWS, 128), f32(SLOTS, ROWS, S),
         jax.ShapeDtypeStruct((FB,), jnp.int32)],
        [vmem(2, UB, ROWS, U), vmem(2, 2, FB, ROWS, S)]
        + [pltpu.SMEM((FB,), jnp.int32)] * 4 + [pltpu.SemaphoreType.DMA((4,))],
        "assemble",
    )(info, placement, held, other, held_sep, sep_other)
    across = lax.ppermute(send, "xhi", swap)
    gathered = lax.all_gather(jnp.stack([send, across]), ("core", "y"), axis=0, tiled=False)
    gathered = gathered.reshape(16, 2, SLOTS, ROWS, S)
    copies = jnp.broadcast_to(upper[None], (16,) + upper.shape)
    copies, _ = lax.optimization_barrier((copies, across))
    all_upper = lax.all_to_all(copies, PANEL, 0, 0, tiled=True)
    inv0, factor0, weight = call(
        first_kernel,
        [SM, VM, VM],
        [f32(S, S), f32(FB, ROWS, S), f32(UB, ROWS, S)],
        [vmem(S, S), vmem(S, S), vmem(128, S)],
        "first",
    )(info, all_upper, pivot)
    gathered = pltpu.with_memory_space_constraint(gathered, pltpu.HBM)
    inv1, strip, cross, picked, turned, trail, kept = call(
        second_kernel,
        [SM, SM, HBM, VM, VM, VM],
        [f32(S, S), f32(SB, ROWS, S), f32(S, S), f32(SB, 128, S), f32(UB * ROWS, S),
         f32(UB * ROWS, U), f32(16, 2, SLOTS, ROWS, S)],
        [vmem(8, 2, SB, ROWS, S), vmem(S, S), vmem(S, S), vmem(128, S), pltpu.SemaphoreType.DMA((88,))],
        "second",
    )(info, following, gathered, front, weight, inv0)
    heads = [(first + 2, first) for first in range(0, 32, 4)]
    sibling = lax.ppermute(trail, LEAF, heads)
    factors, partial = call(
        last_kernel,
        [SM, SM] + [VM] * 9,
        [f32(2, 1, FB, ROWS, S), f32(UB * ROWS, U)],
        [],
        "last",
    )(info, following, kept, front, picked, turned, inv0, cross, inv1, strip, factor0)
    return factors, (partial + sibling).reshape(1, UB, ROWS, U)


def solution(mesh):
    fine = Mesh(mesh.devices.reshape(8, 2, 2, 8, 2), AXES)
    update = P(LEAF, None, PANEL, None)
    columns = P(None, LEAF, None, PANEL, None)
    return jax.shard_map(
        body,
        mesh=fine,
        in_specs=(update, columns, P()),
        out_specs=(columns, update),
        check_vma=False,
    )
```

```python
import jax
import jax.numpy as jnp
from jax import lax
from jax.experimental import pallas as pl
from jax.experimental.pallas import tpu as pltpu
from jax.sharding import Mesh
from jax.sharding import PartitionSpec as P

F = 2048
S = 512
U = 1536
FB = 16
SB = 4
UB = 12
ROWS = 8
SLOTS = 14
BLOCK = 32
HALF = 16
HI = lax.Precision.HIGHEST
AXES = ("z", "xlo", "core", "y", "xhi")
LEAF = ("z", "xlo", "core")
PANEL = ("y", "xhi")
UPPER = [(a, b) for a in range(SB) for b in range(a, SB)]
VMEM_LIMIT = 20 << 20


def nt(a, b):
    return lax.dot_general(
        a, b, (((1,), (1,)), ((), ())), precision=HI, preferred_element_type=jnp.float32
    )


def nn(a, b):
    return jnp.dot(a, b, precision=HI, preferred_element_type=jnp.float32)


def spread_row(tile, row):
    return jnp.broadcast_to(tile[row : row + 1, :], tile.shape)


def split3(x):
    high = x.astype(jnp.bfloat16)
    rest = x - high.astype(jnp.float32)
    mid = rest.astype(jnp.bfloat16)
    low = (rest - mid.astype(jnp.float32)).astype(jnp.bfloat16)
    return high, mid, low


def factor_block(m_ref, start):
    tile, lo = start // 128, start % 128
    groups, cols = BLOCK // 8, S // 128
    lane = lax.broadcasted_iota(jnp.int32, (8, 128), 1)
    sub = lax.broadcasted_iota(jnp.int32, (8, 128), 0)
    rows = [
        [m_ref[start + 8 * g : start + 8 * g + 8, 128 * c : 128 * c + 128] for c in range(cols)]
        for g in range(groups)
    ]
    diag = [rows[g][tile] for g in range(groups)]
    inside = (lane >= lo) & (lane < lo + BLOCK)
    for g in range(groups):
        unit = jnp.where(lane == sub + (lo + 8 * g), 1.0, 0.0)
        rows[g][tile] = jnp.where(inside, unit, diag[g])
    factor = [jnp.zeros((8, 128), jnp.float32) for _ in range(groups)]
    for first in range(0, BLOCK, HALF):
        spread = {
            k: {
                g: jnp.broadcast_to(diag[g][:, lo + k : lo + k + 1], (8, 128))
                for g in range(k // 8, groups)
            }
            for k in range(first, first + HALF)
        }
        last = first + HALF == BLOCK
        for j in range(first, first + HALF):
            gj, s = j // 8, j % 8
            inv = lax.rsqrt(spread_row(spread[j][gj], s))
            col = {g: spread[j][g] * inv for g in range(gj, groups)}
            for k in range(j + 1, first + HALF):
                w = spread_row(col[k // 8], k % 8)
                for g in range(k // 8, groups):
                    spread[k][g] = spread[k][g] - col[g] * w
            below = jnp.where(sub > s, col[gj], 0.0)
            factor[gj] = jnp.where((lane == lo + j) & (sub >= s), col[gj], factor[gj])
            for g in range(gj + 1, groups):
                factor[g] = jnp.where(lane == lo + j, col[g], factor[g])
            for c in range(cols):
                u = spread_row(rows[gj][c], s) * inv
                rows[gj][c] = jnp.where(sub == s, u, rows[gj][c] - below * u)
                for g in range(gj + 1, groups):
                    rows[g][c] = rows[g][c] - col[g] * u
            if not last:
                u = spread_row(diag[gj], s) * inv
                diag[gj] = jnp.where(sub == s, u, diag[gj] - below * u)
                for g in range(gj + 1, groups):
                    diag[g] = diag[g] - col[g] * u
    joined = [jnp.concatenate([rows[g][c] for g in range(groups)], 0) for c in range(cols)]
    return joined, jnp.concatenate(factor, 0)


def factorize(m_ref, l_ref, inv_ref, u_ref):
    cols = S // 128
    lane = lax.broadcasted_iota(jnp.int32, (BLOCK, 128), 1)
    for start in range(0, S, BLOCK):
        end, tile, lo = start + BLOCK, start // 128, start % 128
        rows, diag = factor_block(m_ref, start)
        for c in range(cols):
            if c < tile:
                value = rows[c]
            elif c == tile:
                value = jnp.where(lane < lo + BLOCK, rows[c], 0.0)
            else:
                value = jnp.zeros_like(rows[c])
            inv_ref[start:end, 128 * c : 128 * c + 128] = value
        upper = [jnp.where(lane >= lo + BLOCK, rows[tile], 0.0)] + rows[tile + 1 :]
        for i, value in enumerate(upper):
            c = tile + i
            u_ref[lo : lo + BLOCK, 128 * c : 128 * c + 128] = value
        l_ref[start:end, 128 * tile : 128 * tile + 128] = diag
        if end < S:
            skip = end // 128 - tile
            left = split3(jnp.concatenate(upper[skip:], 1))
            right = split3(jnp.concatenate(rows, 1))
            pairs = ((0, 0), (0, 1), (1, 0), (1, 1), (0, 2), (2, 0))
            update = lax.dot_general(
                jnp.concatenate([left[a] for a, _ in pairs], 0),
                jnp.concatenate([right[b] for _, b in pairs], 0),
                (((0,), (0,)), ((), ())),
                preferred_element_type=jnp.float32,
            )
            offset = end % 128 if skip == 0 else 0
            for c in range(cols):
                value = m_ref[end:S, 128 * c : 128 * c + 128]
                if c == tile:
                    at = lax.broadcasted_iota(jnp.int32, value.shape, 1)
                    value = jnp.where((at >= lo) & (at < lo + BLOCK), 0.0, value)
                m_ref[end:S, 128 * c : 128 * c + 128] = (
                    value - update[offset:, 128 * c : 128 * c + 128]
                )
        if end % 128 == 0:
            at = slice(128 * tile, 128 * tile + 128)
            for c in range(cols):
                if c < tile:
                    l_ref[128 * c : 128 * c + 128, at] = jnp.zeros((128, 128), jnp.float32)
                else:
                    turned = u_ref[:, 128 * c : 128 * c + 128].T
                    if c == tile:
                        turned = turned + l_ref[128 * c : 128 * c + 128, at]
                    l_ref[128 * c : 128 * c + 128, at] = turned


def invert(place_ref, level, leaf, out_ref):
    for t in range(FB):
        out_ref[t] = -1
    for a in range(UB):
        out_ref[place_ref[level, leaf, a]] = a


def assemble_kernel(
    info_ref, place_ref, own_ref, other_ref, sep_own_ref, sep_other_ref,
    pivot_ref, front_ref, upper_ref, send_ref, next_ref,
    child_ref, sep_ref, left_ref, right_ref, from_left_ref, from_right_ref, sems,
):
    leaf, core = info_ref[0], info_ref[2]
    copies = [
        pltpu.make_async_copy(own_ref.at[0], child_ref.at[core], sems.at[0]),
        pltpu.make_async_copy(other_ref, child_ref.at[1 - core], sems.at[1]),
        pltpu.make_async_copy(sep_own_ref.at[:, 0], sep_ref.at[core], sems.at[2]),
        pltpu.make_async_copy(sep_other_ref, sep_ref.at[1 - core], sems.at[3]),
    ]
    for copy in copies:
        copy.start()
    head = leaf - core
    invert(place_ref, 0, head, left_ref)
    invert(place_ref, 0, head + 1, right_ref)
    invert(place_ref, 1, head, next_ref)
    for t in range(FB):
        source = next_ref[t]
        at = jnp.maximum(source, 0) + SB
        from_left_ref[t] = jnp.where(source >= 0, left_ref[at], -1)
        from_right_ref[t] = jnp.where(source >= 0, right_ref[at], -1)
    for copy in copies:
        copy.wait()

    def part(which, row, col):
        at = pl.multiple_of(jnp.maximum(col, 0) * 128, 128)
        value = child_ref[which, jnp.maximum(row, 0), :, pl.ds(at, 128)]
        return jnp.where((row >= 0) & (col >= 0), value, 0.0)

    def pivot_row(t, carry):
        row = left_ref[t]
        for c in range(SB):
            at = slice(128 * c, 128 * c + 128)
            pivot_ref[t, :, at] = part(0, row, left_ref[c]) + sep_ref[0, 0, t, :, at]
        return carry

    lax.fori_loop(0, FB, pivot_row, 0)
    for i, (a, b) in enumerate(UPPER):
        upper_ref[i] = pivot_ref[a, :, 128 * b : 128 * b + 128]

    def front_row(t, carry):
        row_left, row_right = from_left_ref[t], from_right_ref[t]
        for c in range(FB):
            value = part(0, row_left, from_left_ref[c]) + part(1, row_right, from_right_ref[c])
            at = slice(128 * c, 128 * c + 128)
            if c < SB:
                value = value + sep_ref[0, 1, t, :, at]
            front_ref[t, :, at] = value
        return carry

    lax.fori_loop(0, FB, front_row, 0)
    for i in range(UB):
        send_ref[i] = jnp.where(core == 0, pivot_ref[SB + i], front_ref[i, :, :S])
    for i in range(UB, SLOTS):
        send_ref[i] = jnp.where(core == 0, front_ref[i + 2, :, :S], front_ref[i, :, :S])


def first_kernel(
    info_ref, all_upper_ref, pivot_ref,
    inv_ref, factor_ref, weight_ref,
    m_ref, l_ref, u_ref,
):
    for p in range(16):
        for i, (a, b) in enumerate(UPPER):
            row = 128 * a + ROWS * p
            m_ref[row : row + ROWS, 128 * b : 128 * b + 128] = all_upper_ref[p, i]
    factorize(m_ref, l_ref, inv_ref, u_ref)
    panel = info_ref[1]
    heads = info_ref[2] == 0
    inverse = inv_ref[...]
    for a in range(SB):
        row = pl.multiple_of(128 * a + ROWS * panel, ROWS)
        factor_ref[a] = jnp.where(heads, l_ref[pl.ds(row, ROWS), :], 0.0)
    below = nt(pivot_ref[SB:].reshape(UB * ROWS, S), inverse)
    factor_ref[SB:] = jnp.where(heads, below.reshape(UB, ROWS, S), 0.0)
    weight_ref[...] = nn(below, inverse).reshape(UB, ROWS, S)


def strips(ref, base, slot, side):
    sides = (side, 1 - side)
    return jnp.concatenate([ref[base + y, sides[x], slot] for y in range(8) for x in range(2)], 0)


def second_kernel(
    info_ref, next_ref, all_ref, front_ref, weight_ref, inv_before_ref,
    inv_ref, strip_ref, cross_ref, x_ref, w_ref, trail_ref,
    kept_ref, p_ref, m_ref, l_ref, u_ref, sems,
):
    side = info_ref[3]
    first = []
    for y in range(8):
        first.append(
            pltpu.make_async_copy(all_ref.at[8 + y, :, pl.ds(0, SB)], p_ref.at[y], sems.at[len(first)])
        )
    for t in range(SB):
        source = jnp.maximum(next_ref[t], 0)
        for y in range(8):
            for other in range(2):
                at = 2 * y + (side if other == 0 else 1 - side)
                row = pl.multiple_of(at * ROWS, ROWS)
                first.append(
                    pltpu.make_async_copy(
                        all_ref.at[y, other, source],
                        x_ref.at[t, pl.ds(row, ROWS)],
                        sems.at[len(first)],
                    )
                )
    rest = [
        pltpu.make_async_copy(all_ref.at[i], kept_ref.at[i], sems.at[len(first) + i])
        for i in range(8)
    ]
    for copy in first:
        copy.start()
    for t in range(UB):
        source = next_ref[SB + t]
        moved = weight_ref[jnp.maximum(source, 0)]
        w_ref[ROWS * t : ROWS * t + ROWS, :] = jnp.where(source >= 0, moved, 0.0)
    for copy in first:
        copy.wait()
    heads = (info_ref[0] - info_ref[2]) % 4 == 0

    @pl.when(heads)
    def _():
        for t in range(SB):
            x_ref[t] = jnp.where(next_ref[t] >= 0, x_ref[t], 0.0)
        cross = nt(x_ref[...].reshape(S, S), inv_before_ref[...])
        cross_ref[...] = cross
        product = nt(cross, cross)
        for a in range(SB):
            at = slice(128 * a, 128 * a + 128)
            m_ref[at, :] = strips(p_ref, 0, a, side) - product[at, :]
        factorize(m_ref, l_ref, inv_ref, u_ref)
        for a in range(SB):
            row = pl.multiple_of(128 * a + ROWS * info_ref[1], ROWS)
            strip_ref[a] = l_ref[pl.ds(row, ROWS), :]

    @pl.when(jnp.logical_not(heads))
    def _():
        for copy in rest:
            copy.start()
        weight = w_ref[...]
        for copy in rest:
            copy.wait()
        for t in range(UB):
            source = next_ref[SB + t]
            x = strips(kept_ref, 0, jnp.maximum(source, 0), side)
            old = front_ref[SB:, :, S + 128 * t : S + 128 * t + 128].reshape(UB * ROWS, 128)
            product = jnp.where(source >= 0, nt(x, weight).T, 0.0)
            trail_ref[:, 128 * t : 128 * t + 128] = old - product


def last_kernel(
    info_ref, next_ref, all_ref, front_ref, x_ref, w_ref, inv_before_ref, cross_ref,
    inv_ref, strip_ref, factor_ref,
    factors_ref, part_ref,
    kept_ref, sems,
):
    side = info_ref[3]
    heads = info_ref[0] % 4 == 0
    factors_ref[0, 0] = factor_ref[...]

    @pl.when(heads)
    def _():
        copies = [
            pltpu.make_async_copy(all_ref.at[i], kept_ref.at[i], sems.at[i]) for i in range(16)
        ]
        for copy in copies:
            copy.start()
        inverse = inv_ref[...]
        before = w_ref[...]
        pivots = front_ref[SB:, :, :S].reshape(UB * ROWS, S) - nt(before, x_ref[...].reshape(S, S))
        below = nt(pivots, inverse)
        factors_ref[1, 0, :SB] = strip_ref[...]
        factors_ref[1, 0, SB:] = below.reshape(UB, ROWS, S)
        weight = nn(below, inverse)
        mixed = before - nn(nn(weight, cross_ref[...]), inv_before_ref[...])
        for copy in copies:
            copy.wait()
        for t in range(UB):
            source = next_ref[SB + t]
            block = SB + t
            if block < SLOTS:
                p = strips(kept_ref, 8, block, side)
            else:
                p = strips(kept_ref, 0, block - 2, side)
            x = strips(kept_ref, 0, jnp.maximum(source, 0), side)
            old = front_ref[SB:, :, S + 128 * t : S + 128 * t + 128].reshape(UB * ROWS, 128)
            value = old - nt(p, weight).T - jnp.where(source >= 0, nt(x, mixed).T, 0.0)
            part_ref[:, 128 * t : 128 * t + 128] = value

    @pl.when(jnp.logical_not(heads))
    def _():
        factors_ref[1, 0] = jnp.zeros((FB, ROWS, S), jnp.float32)
        part_ref[...] = jnp.zeros((UB * ROWS, U), jnp.float32)


VM = pl.BlockSpec(memory_space=pltpu.VMEM)
SM = pl.BlockSpec(memory_space=pltpu.SMEM)
HBM = pl.BlockSpec(memory_space=pltpu.HBM)


def f32(*shape):
    return jax.ShapeDtypeStruct(shape, jnp.float32)


def call(kernel, ins, outs, scratch, name):
    return pl.pallas_call(
        kernel,
        in_specs=ins,
        out_specs=[SM if out.dtype == jnp.int32 else VM for out in outs],
        out_shape=outs,
        scratch_shapes=scratch,
        compiler_params=pltpu.CompilerParams(vmem_limit_bytes=VMEM_LIMIT),
        name=name,
    )


def vmem(*shape):
    return pltpu.VMEM(shape, jnp.float32)


def body(child_update, separator_columns, placement):
    leaf = lax.axis_index(LEAF)
    panel = lax.axis_index(PANEL)
    core = lax.axis_index("core")
    xhi = lax.axis_index("xhi")
    info = jnp.stack([leaf, panel, core, xhi]).astype(jnp.int32)
    swap = [(0, 1), (1, 0)]
    other = lax.ppermute(child_update[0], "core", swap)
    sep_other = lax.ppermute(separator_columns[:, 0], "core", swap)
    held = pltpu.with_memory_space_constraint(child_update, pltpu.HBM)
    held_sep = pltpu.with_memory_space_constraint(separator_columns, pltpu.HBM)
    pivot, front, upper, send, following = call(
        assemble_kernel,
        [SM, SM, HBM, HBM, HBM, HBM],
        [f32(FB, ROWS, S), f32(FB, ROWS, F), f32(len(UPPER), ROWS, 128), f32(SLOTS, ROWS, S),
         jax.ShapeDtypeStruct((FB,), jnp.int32)],
        [vmem(2, UB, ROWS, U), vmem(2, 2, FB, ROWS, S)]
        + [pltpu.SMEM((FB,), jnp.int32)] * 4 + [pltpu.SemaphoreType.DMA((4,))],
        "assemble",
    )(info, placement, held, other, held_sep, sep_other)
    across = lax.ppermute(send, "xhi", swap)
    gathered = lax.all_gather(jnp.stack([send, across]), ("core", "y"), axis=0, tiled=False)
    gathered = gathered.reshape(16, 2, SLOTS, ROWS, S)
    copies = jnp.broadcast_to(upper[None], (16,) + upper.shape)
    copies, _ = lax.optimization_barrier((copies, across))
    all_upper = lax.all_to_all(copies, PANEL, 0, 0, tiled=True)
    inv0, factor0, weight = call(
        first_kernel,
        [SM, VM, VM],
        [f32(S, S), f32(FB, ROWS, S), f32(UB, ROWS, S)],
        [vmem(S, S), vmem(S, S), vmem(128, S)],
        "first",
    )(info, all_upper, pivot)
    gathered = pltpu.with_memory_space_constraint(gathered, pltpu.HBM)
    inv1, strip, cross, picked, turned, trail = call(
        second_kernel,
        [SM, SM, HBM, VM, VM, VM],
        [f32(S, S), f32(SB, ROWS, S), f32(S, S), f32(SB, 128, S), f32(UB * ROWS, S),
         f32(UB * ROWS, U)],
        [vmem(8, 2, SLOTS, ROWS, S), vmem(8, 2, SB, ROWS, S), vmem(S, S), vmem(S, S), vmem(128, S), pltpu.SemaphoreType.DMA((80,))],
        "second",
    )(info, following, gathered, front, weight, inv0)
    heads = [(first + 2, first) for first in range(0, 32, 4)]
    sibling = lax.ppermute(trail, LEAF, heads)
    factors, partial = call(
        last_kernel,
        [SM, SM, HBM] + [VM] * 8,
        [f32(2, 1, FB, ROWS, S), f32(UB * ROWS, U)],
        [vmem(16, 2, SLOTS, ROWS, S), pltpu.SemaphoreType.DMA((16,))],
        "last",
    )(info, following, gathered, front, picked, turned, inv0, cross, inv1, strip, factor0)
    return factors, (partial + sibling).reshape(1, UB, ROWS, U)


def solution(mesh):
    fine = Mesh(mesh.devices.reshape(8, 2, 2, 8, 2), AXES)
    update = P(LEAF, None, PANEL, None)
    columns = P(None, LEAF, None, PANEL, None)
    return jax.shard_map(
        body,
        mesh=fine,
        in_specs=(update, columns, P()),
        out_specs=(columns, update),
        check_vma=False,
    )
```

```python
import jax
import jax.numpy as jnp
from jax import lax
from jax.experimental import pallas as pl
from jax.experimental.pallas import tpu as pltpu
from jax.sharding import Mesh
from jax.sharding import PartitionSpec as P

F = 2048
S = 512
U = 1536
FB = 16
SB = 4
UB = 12
ROWS = 8
SLOTS = 14
BLOCK = 32
HALF = 16
HI = lax.Precision.HIGHEST
AXES = ("z", "xlo", "core", "y", "xhi")
LEAF = ("z", "xlo", "core")
PANEL = ("y", "xhi")
UPPER = [(a, b) for a in range(SB) for b in range(a, SB)]
VMEM_LIMIT = 20 << 20


def nt(a, b):
    return lax.dot_general(
        a, b, (((1,), (1,)), ((), ())), precision=HI, preferred_element_type=jnp.float32
    )


def nn(a, b):
    return jnp.dot(a, b, precision=HI, preferred_element_type=jnp.float32)


def spread_row(tile, row):
    return jnp.broadcast_to(tile[row : row + 1, :], tile.shape)


def split3(x):
    high = x.astype(jnp.bfloat16)
    rest = x - high.astype(jnp.float32)
    mid = rest.astype(jnp.bfloat16)
    low = (rest - mid.astype(jnp.float32)).astype(jnp.bfloat16)
    return high, mid, low


def factor_block(m_ref, start):
    tile, lo = start // 128, start % 128
    groups, cols = BLOCK // 8, S // 128
    lane = lax.broadcasted_iota(jnp.int32, (8, 128), 1)
    sub = lax.broadcasted_iota(jnp.int32, (8, 128), 0)
    rows = [
        [m_ref[start + 8 * g : start + 8 * g + 8, 128 * c : 128 * c + 128] for c in range(cols)]
        for g in range(groups)
    ]
    diag = [rows[g][tile] for g in range(groups)]
    inside = (lane >= lo) & (lane < lo + BLOCK)
    for g in range(groups):
        unit = jnp.where(lane == sub + (lo + 8 * g), 1.0, 0.0)
        rows[g][tile] = jnp.where(inside, unit, diag[g])
    factor = [jnp.zeros((8, 128), jnp.float32) for _ in range(groups)]
    for first in range(0, BLOCK, HALF):
        spread = {
            k: {
                g: jnp.broadcast_to(diag[g][:, lo + k : lo + k + 1], (8, 128))
                for g in range(k // 8, groups)
            }
            for k in range(first, first + HALF)
        }
        last = first + HALF == BLOCK
        for j in range(first, first + HALF):
            gj, s = j // 8, j % 8
            inv = lax.rsqrt(spread_row(spread[j][gj], s))
            col = {g: spread[j][g] * inv for g in range(gj, groups)}
            for k in range(j + 1, first + HALF):
                w = spread_row(col[k // 8], k % 8)
                for g in range(k // 8, groups):
                    spread[k][g] = spread[k][g] - col[g] * w
            below = jnp.where(sub > s, col[gj], 0.0)
            factor[gj] = jnp.where((lane == lo + j) & (sub >= s), col[gj], factor[gj])
            for g in range(gj + 1, groups):
                factor[g] = jnp.where(lane == lo + j, col[g], factor[g])
            for c in range(cols):
                u = spread_row(rows[gj][c], s) * inv
                rows[gj][c] = jnp.where(sub == s, u, rows[gj][c] - below * u)
                for g in range(gj + 1, groups):
                    rows[g][c] = rows[g][c] - col[g] * u
            if not last:
                u = spread_row(diag[gj], s) * inv
                diag[gj] = jnp.where(sub == s, u, diag[gj] - below * u)
                for g in range(gj + 1, groups):
                    diag[g] = diag[g] - col[g] * u
    joined = [jnp.concatenate([rows[g][c] for g in range(groups)], 0) for c in range(cols)]
    return joined, jnp.concatenate(factor, 0)


def factorize(m_ref, l_ref, inv_ref, u_ref):
    cols = S // 128
    lane = lax.broadcasted_iota(jnp.int32, (BLOCK, 128), 1)
    for start in range(0, S, BLOCK):
        end, tile, lo = start + BLOCK, start // 128, start % 128
        rows, diag = factor_block(m_ref, start)
        for c in range(cols):
            if c < tile:
                value = rows[c]
            elif c == tile:
                value = jnp.where(lane < lo + BLOCK, rows[c], 0.0)
            else:
                value = jnp.zeros_like(rows[c])
            inv_ref[start:end, 128 * c : 128 * c + 128] = value
        upper = [jnp.where(lane >= lo + BLOCK, rows[tile], 0.0)] + rows[tile + 1 :]
        for i, value in enumerate(upper):
            c = tile + i
            u_ref[lo : lo + BLOCK, 128 * c : 128 * c + 128] = value
        l_ref[start:end, 128 * tile : 128 * tile + 128] = diag
        if end < S:
            skip = end // 128 - tile
            left = split3(jnp.concatenate(upper[skip:], 1))
            right = split3(jnp.concatenate(rows, 1))
            pairs = ((0, 0), (0, 1), (1, 0), (1, 1), (0, 2), (2, 0))
            update = lax.dot_general(
                jnp.concatenate([left[a] for a, _ in pairs], 0),
                jnp.concatenate([right[b] for _, b in pairs], 0),
                (((0,), (0,)), ((), ())),
                preferred_element_type=jnp.float32,
            )
            offset = end % 128 if skip == 0 else 0
            for c in range(cols):
                value = m_ref[end:S, 128 * c : 128 * c + 128]
                if c == tile:
                    at = lax.broadcasted_iota(jnp.int32, value.shape, 1)
                    value = jnp.where((at >= lo) & (at < lo + BLOCK), 0.0, value)
                m_ref[end:S, 128 * c : 128 * c + 128] = (
                    value - update[offset:, 128 * c : 128 * c + 128]
                )
        if end % 128 == 0:
            at = slice(128 * tile, 128 * tile + 128)
            for c in range(cols):
                if c < tile:
                    l_ref[128 * c : 128 * c + 128, at] = jnp.zeros((128, 128), jnp.float32)
                else:
                    turned = u_ref[:, 128 * c : 128 * c + 128].T
                    if c == tile:
                        turned = turned + l_ref[128 * c : 128 * c + 128, at]
                    l_ref[128 * c : 128 * c + 128, at] = turned


def invert(place_ref, level, leaf, out_ref):
    for t in range(FB):
        out_ref[t] = -1
    for a in range(UB):
        out_ref[place_ref[level, leaf, a]] = a


def assemble_kernel(
    info_ref, place_ref, own_ref, other_ref, sep_own_ref, sep_other_ref,
    pivot_ref, front_ref, upper_ref, send_ref, next_ref,
    child_ref, sep_ref, left_ref, right_ref, from_left_ref, from_right_ref, sems,
):
    leaf, core = info_ref[0], info_ref[2]
    copies = [
        pltpu.make_async_copy(own_ref.at[0], child_ref.at[core], sems.at[0]),
        pltpu.make_async_copy(other_ref, child_ref.at[1 - core], sems.at[1]),
        pltpu.make_async_copy(sep_own_ref.at[:, 0], sep_ref.at[core], sems.at[2]),
        pltpu.make_async_copy(sep_other_ref, sep_ref.at[1 - core], sems.at[3]),
    ]
    for copy in copies:
        copy.start()
    head = leaf - core
    invert(place_ref, 0, head, left_ref)
    invert(place_ref, 0, head + 1, right_ref)
    invert(place_ref, 1, head, next_ref)
    for t in range(FB):
        source = next_ref[t]
        at = jnp.maximum(source, 0) + SB
        from_left_ref[t] = jnp.where(source >= 0, left_ref[at], -1)
        from_right_ref[t] = jnp.where(source >= 0, right_ref[at], -1)
    for copy in copies:
        copy.wait()

    def part(which, row, col):
        at = pl.multiple_of(jnp.maximum(col, 0) * 128, 128)
        value = child_ref[which, jnp.maximum(row, 0), :, pl.ds(at, 128)]
        return jnp.where((row >= 0) & (col >= 0), value, 0.0)

    def pivot_row(t, carry):
        row = left_ref[t]
        for c in range(SB):
            at = slice(128 * c, 128 * c + 128)
            pivot_ref[t, :, at] = part(0, row, left_ref[c]) + sep_ref[0, 0, t, :, at]
        return carry

    lax.fori_loop(0, FB, pivot_row, 0)
    for i, (a, b) in enumerate(UPPER):
        upper_ref[i] = pivot_ref[a, :, 128 * b : 128 * b + 128]

    def front_row(t, carry):
        row_left, row_right = from_left_ref[t], from_right_ref[t]
        for c in range(FB):
            value = part(0, row_left, from_left_ref[c]) + part(1, row_right, from_right_ref[c])
            at = slice(128 * c, 128 * c + 128)
            if c < SB:
                value = value + sep_ref[0, 1, t, :, at]
            front_ref[t, :, at] = value
        return carry

    lax.fori_loop(0, FB, front_row, 0)
    for i in range(UB):
        send_ref[i] = jnp.where(core == 0, pivot_ref[SB + i], front_ref[i, :, :S])
    for i in range(UB, SLOTS):
        send_ref[i] = jnp.where(core == 0, front_ref[i + 2, :, :S], front_ref[i, :, :S])


def first_kernel(
    info_ref, all_upper_ref, pivot_ref,
    inv_ref, factor_ref, weight_ref,
    m_ref, l_ref, u_ref,
):
    for p in range(16):
        for i, (a, b) in enumerate(UPPER):
            row = 128 * a + ROWS * p
            m_ref[row : row + ROWS, 128 * b : 128 * b + 128] = all_upper_ref[p, i]
    factorize(m_ref, l_ref, inv_ref, u_ref)
    panel = info_ref[1]
    heads = info_ref[2] == 0
    inverse = inv_ref[...]
    for a in range(SB):
        row = pl.multiple_of(128 * a + ROWS * panel, ROWS)
        factor_ref[a] = jnp.where(heads, l_ref[pl.ds(row, ROWS), :], 0.0)
    below = nt(pivot_ref[SB:].reshape(UB * ROWS, S), inverse)
    factor_ref[SB:] = jnp.where(heads, below.reshape(UB, ROWS, S), 0.0)
    weight_ref[...] = nn(below, inverse).reshape(UB, ROWS, S)


def strips(ref, base, slot, side):
    sides = (side, 1 - side)
    return jnp.concatenate([ref[base + y, sides[x], slot] for y in range(8) for x in range(2)], 0)


def update_kernel(
    info_ref, next_ref, all_ref, front_ref, weight_ref,
    w_ref, trail_ref,
    kept_ref, sems,
):
    for t in range(UB):
        source = next_ref[SB + t]
        moved = weight_ref[jnp.maximum(source, 0)]
        w_ref[ROWS * t : ROWS * t + ROWS, :] = jnp.where(source >= 0, moved, 0.0)
    heads = (info_ref[0] - info_ref[2]) % 4 == 0

    @pl.when(jnp.logical_not(heads))
    def _():
        copies = [
            pltpu.make_async_copy(all_ref.at[i], kept_ref.at[i], sems.at[i]) for i in range(8)
        ]
        for copy in copies:
            copy.start()
        weight = w_ref[...]
        for copy in copies:
            copy.wait()
        for t in range(UB):
            source = next_ref[SB + t]
            x = strips(kept_ref, 0, jnp.maximum(source, 0), info_ref[3])
            old = front_ref[SB:, :, S + 128 * t : S + 128 * t + 128].reshape(UB * ROWS, 128)
            product = jnp.where(source >= 0, nt(x, weight).T, 0.0)
            trail_ref[:, 128 * t : 128 * t + 128] = old - product


def second_kernel(
    info_ref, next_ref, all_ref, inv_before_ref,
    inv_ref, strip_ref, cross_ref, x_ref,
    p_ref, m_ref, l_ref, u_ref, sems,
):
    side = info_ref[3]
    copies = []
    for y in range(8):
        copies.append(
            pltpu.make_async_copy(all_ref.at[8 + y, :, pl.ds(0, SB)], p_ref.at[y], sems.at[len(copies)])
        )
    for t in range(SB):
        source = jnp.maximum(next_ref[t], 0)
        for y in range(8):
            for other in range(2):
                at = 2 * y + (side if other == 0 else 1 - side)
                row = pl.multiple_of(at * ROWS, ROWS)
                copies.append(
                    pltpu.make_async_copy(
                        all_ref.at[y, other, source],
                        x_ref.at[t, pl.ds(row, ROWS)],
                        sems.at[len(copies)],
                    )
                )
    for copy in copies:
        copy.start()
    for copy in copies:
        copy.wait()
    for t in range(SB):
        x_ref[t] = jnp.where(next_ref[t] >= 0, x_ref[t], 0.0)
    cross = nt(x_ref[...].reshape(S, S), inv_before_ref[...])
    cross_ref[...] = cross
    product = nt(cross, cross)
    for a in range(SB):
        at = slice(128 * a, 128 * a + 128)
        m_ref[at, :] = strips(p_ref, 0, a, side) - product[at, :]
    factorize(m_ref, l_ref, inv_ref, u_ref)
    for a in range(SB):
        row = pl.multiple_of(128 * a + ROWS * info_ref[1], ROWS)
        strip_ref[a] = l_ref[pl.ds(row, ROWS), :]


def last_kernel(
    info_ref, next_ref, all_ref, front_ref, x_ref, w_ref, inv_before_ref, cross_ref,
    inv_ref, strip_ref, factor_ref,
    factors_ref, part_ref,
    kept_ref, sems,
):
    side = info_ref[3]
    heads = info_ref[0] % 4 == 0
    factors_ref[0, 0] = factor_ref[...]

    @pl.when(heads)
    def _():
        copies = [
            pltpu.make_async_copy(all_ref.at[i], kept_ref.at[i], sems.at[i]) for i in range(16)
        ]
        for copy in copies:
            copy.start()
        inverse = inv_ref[...]
        before = w_ref[...]
        pivots = front_ref[SB:, :, :S].reshape(UB * ROWS, S) - nt(before, x_ref[...].reshape(S, S))
        below = nt(pivots, inverse)
        factors_ref[1, 0, :SB] = strip_ref[...]
        factors_ref[1, 0, SB:] = below.reshape(UB, ROWS, S)
        weight = nn(below, inverse)
        mixed = before - nn(nn(weight, cross_ref[...]), inv_before_ref[...])
        for copy in copies:
            copy.wait()
        for t in range(UB):
            source = next_ref[SB + t]
            block = SB + t
            if block < SLOTS:
                p = strips(kept_ref, 8, block, side)
            else:
                p = strips(kept_ref, 0, block - 2, side)
            x = strips(kept_ref, 0, jnp.maximum(source, 0), side)
            old = front_ref[SB:, :, S + 128 * t : S + 128 * t + 128].reshape(UB * ROWS, 128)
            value = old - nt(p, weight).T - jnp.where(source >= 0, nt(x, mixed).T, 0.0)
            part_ref[:, 128 * t : 128 * t + 128] = value

    @pl.when(jnp.logical_not(heads))
    def _():
        factors_ref[1, 0] = jnp.zeros((FB, ROWS, S), jnp.float32)
        part_ref[...] = jnp.zeros((UB * ROWS, U), jnp.float32)


VM = pl.BlockSpec(memory_space=pltpu.VMEM)
SM = pl.BlockSpec(memory_space=pltpu.SMEM)
HBM = pl.BlockSpec(memory_space=pltpu.HBM)


def f32(*shape):
    return jax.ShapeDtypeStruct(shape, jnp.float32)


def call(kernel, ins, outs, scratch, name):
    return pl.pallas_call(
        kernel,
        in_specs=ins,
        out_specs=[SM if out.dtype == jnp.int32 else VM for out in outs],
        out_shape=outs,
        scratch_shapes=scratch,
        compiler_params=pltpu.CompilerParams(vmem_limit_bytes=VMEM_LIMIT),
        name=name,
    )


def vmem(*shape):
    return pltpu.VMEM(shape, jnp.float32)


def body(child_update, separator_columns, placement):
    leaf = lax.axis_index(LEAF)
    panel = lax.axis_index(PANEL)
    core = lax.axis_index("core")
    xhi = lax.axis_index("xhi")
    info = jnp.stack([leaf, panel, core, xhi]).astype(jnp.int32)
    swap = [(0, 1), (1, 0)]
    other = lax.ppermute(child_update[0], "core", swap)
    sep_other = lax.ppermute(separator_columns[:, 0], "core", swap)
    held = pltpu.with_memory_space_constraint(child_update, pltpu.HBM)
    held_sep = pltpu.with_memory_space_constraint(separator_columns, pltpu.HBM)
    pivot, front, upper, send, following = call(
        assemble_kernel,
        [SM, SM, HBM, HBM, HBM, HBM],
        [f32(FB, ROWS, S), f32(FB, ROWS, F), f32(len(UPPER), ROWS, 128), f32(SLOTS, ROWS, S),
         jax.ShapeDtypeStruct((FB,), jnp.int32)],
        [vmem(2, UB, ROWS, U), vmem(2, 2, FB, ROWS, S)]
        + [pltpu.SMEM((FB,), jnp.int32)] * 4 + [pltpu.SemaphoreType.DMA((4,))],
        "assemble",
    )(info, placement, held, other, held_sep, sep_other)
    across = lax.ppermute(send, "xhi", swap)
    gathered = lax.all_gather(jnp.stack([send, across]), ("core", "y"), axis=0, tiled=False)
    gathered = gathered.reshape(16, 2, SLOTS, ROWS, S)
    copies = jnp.broadcast_to(upper[None], (16,) + upper.shape)
    copies, _ = lax.optimization_barrier((copies, across))
    all_upper = lax.all_to_all(copies, PANEL, 0, 0, tiled=True)
    inv0, factor0, weight = call(
        first_kernel,
        [SM, VM, VM],
        [f32(S, S), f32(FB, ROWS, S), f32(UB, ROWS, S)],
        [vmem(S, S), vmem(S, S), vmem(128, S)],
        "first",
    )(info, all_upper, pivot)
    gathered = pltpu.with_memory_space_constraint(gathered, pltpu.HBM)
    turned, trail = call(
        update_kernel,
        [SM, SM, HBM, VM, VM],
        [f32(UB * ROWS, S), f32(UB * ROWS, U)],
        [vmem(8, 2, SLOTS, ROWS, S), pltpu.SemaphoreType.DMA((8,))],
        "update",
    )(info, following, gathered, front, weight)
    heads = [(first + 2, first) for first in range(0, 32, 4)]
    sibling = lax.ppermute(trail, LEAF, heads)
    inv1, strip, cross, picked = call(
        second_kernel,
        [SM, SM, HBM, VM],
        [f32(S, S), f32(SB, ROWS, S), f32(S, S), f32(SB, 128, S)],
        [vmem(8, 2, SB, ROWS, S), vmem(S, S), vmem(S, S), vmem(128, S), pltpu.SemaphoreType.DMA((72,))],
        "second",
    )(info, following, gathered, inv0)
    factors, partial = call(
        last_kernel,
        [SM, SM, HBM] + [VM] * 8,
        [f32(2, 1, FB, ROWS, S), f32(UB * ROWS, U)],
        [vmem(16, 2, SLOTS, ROWS, S), pltpu.SemaphoreType.DMA((16,))],
        "last",
    )(info, following, gathered, front, picked, turned, inv0, cross, inv1, strip, factor0)
    return factors, (partial + sibling).reshape(1, UB, ROWS, U)


def solution(mesh):
    fine = Mesh(mesh.devices.reshape(8, 2, 2, 8, 2), AXES)
    update = P(LEAF, None, PANEL, None)
    columns = P(None, LEAF, None, PANEL, None)
    return jax.shard_map(
        body,
        mesh=fine,
        in_specs=(update, columns, P()),
        out_specs=(columns, update),
        check_vma=False,
    )
```
